256 devices in a mesh: region: 32 (over y, z), feat: 8 (over x, core).
Axes of the slice: x: 4, y: 4, z: 8, core: 2. Of those that a mesh axis runs over, the one named last changes fastest.
Arguments:
- enc_feat: bfloat16 [128, 131072], P('feat', 'region'), may hold values from -6 to 6
- send_order: int32 [32, 32], P('region'), may hold values from 0 to 31, each once within a row
- recv_slot: int32 [32, 32], P('region'), may hold values from 0 to 31, each once within a row
- want: int32 [32, 32, 4], P('region'), may hold values from 0 to 15
- neighbours: int32 [1024, 8], P('region'), may hold values from 0 to 159, as said below
- edge_src: int32 [1024, 8, 128], P('region'), may hold values from 0 to 127
- edge_dst: int32 [1024, 8, 128], P('region'), may hold values from 0 to 127
- conductance: bfloat16 [1024, 8, 128], P('region'), may hold values from 0.049804688 to 0.5
- w_in_h: bfloat16 [2, 128, 128], P(None, 'feat'), may hold values from -0.375 to 0.375
- w_in_m: bfloat16 [2, 128, 128], P(None, 'feat'), may hold values from -0.375 to 0.375
- bias_in: float32 [2, 128], P(None, 'feat'), may hold values from -3 to 3
- w_out: bfloat16 [2, 128, 128], P(None, None, 'feat'), may hold values from -0.5 to 0.5
- ln_gain: float32 [2, 128], P(None, 'feat'), may hold values from 0.1 to 1.9
- ln_shift: float32 [2, 128], P(None, 'feat'), may hold values from -2 to 2
- w_read: float32 [128], P('feat'), may hold values from -0.5 to 0.5
Outputs:
- hidden: bfloat16 [128, 131072], P('feat', 'region')
- pressure: float32 [131072], P('region')
The draws below stay inside these ranges and needn't reach their ends.
Inputs may be any that keep to these rules, and one draw needn't show every extreme that they name: `neighbours`: entry 0 of a block is its own slot within its partition; an entry below 32 is a block of the same partition; an entry 32 + s * 4 + c names panel c that this partition takes from partition s. `send_order`: each row is a permutation of the brick owner's local blocks. `recv_slot`: each row is a permutation of the partition's local slots.
All inputs are finite; a program needn't handle non-finite values.
Results may differ from the reference program's by a relative error of at most 0.0056.
Values may be sent and summed in bfloat16 or wider, within the bound.
A program may use at most 64 MiB of HBM per device.

```python
import math
import jax
import jax.numpy as jnp
from jax import lax

WIDTH = 128
MLP_HID = 128
BLOCK = 128
BLK_DEV = 32
NBR = 8
EDGES = 128
EXPORT = 16
CAPACITY = 4
LAYERS = 2
REGIONS = 32
BLOCKS = 1024
NODES = 131072


def draw_neighbours(key, part):
    key = jax.random.fold_in(key, 7)
    key_near, key_far, key_pick = jax.random.split(key, 3)
    rows = jnp.arange(BLOCKS, dtype=jnp.int32)
    local_row = rows % BLK_DEV
    near = jax.random.randint(key_near, (BLOCKS, NBR), 0, BLK_DEV)
    far = BLK_DEV + jax.random.randint(key_far, (BLOCKS, NBR), 0, REGIONS * CAPACITY)
    pick = jax.random.randint(key_pick, (BLOCKS, NBR), 0, 2)
    table = jnp.where(pick == 1, far, near)
    table = table.at[:, 0].set(local_row)
    last_col = jnp.where(local_row == BLK_DEV - 1, BLK_DEV + REGIONS * CAPACITY - 1, table[:, NBR - 1])
    table = table.at[:, NBR - 1].set(last_col)
    return table.astype(jnp.int32)


def set_ends(values, rng, least, top_value):
    longest = values.shape.index(max(values.shape))
    spots = []
    for shift in (0, 1):
        where = [jax.random.randint(jax.random.fold_in(rng, axis), (), 0, length) for axis, length in enumerate(values.shape)]
        where[longest] = (where[longest] + shift) % values.shape[longest]
        spots.append(tuple(where))
    return values.at[spots[0]].set(least).at[spots[1]].set(top_value)


def steps_of(rng, dims, cuts, low, largest):
    factor_of = 1.0
    for axis_at, blocks in cuts:
        draws = jax.random.uniform(jax.random.fold_in(jax.random.fold_in(rng, 6), axis_at), (blocks,), jnp.float32, low / len(cuts), largest / len(cuts))
        factor_of = factor_of * jnp.repeat(jnp.exp(draws), dims[axis_at] // blocks).reshape((-1,) + (1,) * (len(dims) - 1 - axis_at))
    return factor_of


def scatter_about(rng, extent, scale, reach, cuts=(), kind=jnp.bfloat16):
    array = scale * jax.random.normal(rng, extent, jnp.float32)
    if cuts:
        array = array * steps_of(rng, extent, cuts, -0.22, 0.18)
    return jnp.clip(array, -reach, reach).astype(kind)


def setup_inputs(seed: int = 0) -> dict:
    keys = jax.random.split(jax.random.key(seed), 16)
    return {
        "enc_feat": scatter_about(keys[0], (WIDTH, NODES), 1.0, 6.0, ((0, 8), (1, 32))),
        "send_order": jax.vmap(lambda own: jax.random.permutation(own, BLK_DEV))(jax.random.split(keys[1], REGIONS)).reshape((REGIONS, BLK_DEV)).astype(jnp.int32),
        "recv_slot": jax.vmap(lambda own: jax.random.permutation(own, BLK_DEV))(jax.random.split(keys[2], REGIONS)).reshape((REGIONS, BLK_DEV)).astype(jnp.int32),
        "want": set_ends(jax.random.randint(keys[3], (REGIONS, REGIONS, CAPACITY), 0, EXPORT), jax.random.fold_in(keys[3], 1), 0, EXPORT - 1).astype(jnp.int32),
        "neighbours": draw_neighbours(jax.random.fold_in(keys[15], 71), 0),
        "edge_src": set_ends(jax.random.randint(keys[5], (BLOCKS, NBR, EDGES), 0, BLOCK), jax.random.fold_in(keys[5], 1), 0, BLOCK - 1).astype(jnp.int32),
        "edge_dst": set_ends(jax.random.randint(keys[6], (BLOCKS, NBR, EDGES), 0, BLOCK), jax.random.fold_in(keys[6], 1), 0, BLOCK - 1).astype(jnp.int32),
        "conductance": jnp.clip(jnp.exp(math.log(0.5) - 2.306499 * jax.random.uniform(keys[7], (BLOCKS, NBR, EDGES), jnp.float32) ** steps_of(keys[7], (BLOCKS, NBR, EDGES), ((0, 32),), -0.2, 0.2)), 0.049804688, 0.5).astype(jnp.bfloat16),
        "w_in_h": scatter_about(keys[8], (LAYERS, MLP_HID, WIDTH), (2 * WIDTH) ** -0.5, 0.375, ((1, 8),)),
        "w_in_m": scatter_about(keys[9], (LAYERS, MLP_HID, WIDTH), (2 * WIDTH) ** -0.5, 0.375, ((1, 8),)),
        "bias_in": scatter_about(keys[10], (LAYERS, MLP_HID), 0.5, 3.0, ((1, 8),), jnp.float32),
        "w_out": scatter_about(keys[11], (LAYERS, WIDTH, MLP_HID), MLP_HID ** -0.5, 0.5, ((2, 8),)),
        "ln_gain": jnp.clip(1.0 + 0.18 * jax.random.normal(keys[12], (LAYERS, WIDTH), jnp.float32), 0.1, 1.9),
        "ln_shift": scatter_about(keys[13], (LAYERS, WIDTH), 0.3, 2.0, ((1, 8),), jnp.float32),
        "w_read": scatter_about(keys[14], (WIDTH,), WIDTH ** -0.5, 0.5, ((0, 8),), jnp.float32),
    }


def neighbour_blocks(want, neighbours):
    rows = jnp.arange(BLOCKS, dtype=jnp.int32)
    owner = rows // BLK_DEV
    columns = []
    for column in range(NBR):
        entry = neighbours[:, column]
        offset = jnp.maximum(entry - BLK_DEV, 0)
        source = offset // CAPACITY
        panel = offset % CAPACITY
        remote = source * BLK_DEV + (BLK_DEV - EXPORT) + want[owner, source, panel]
        columns.append(jnp.where(entry < BLK_DEV, owner * BLK_DEV + entry, remote))
    return jnp.stack(columns, axis=1).astype(jnp.int32)

def reference(enc_feat, send_order, recv_slot, want, neighbours, edge_src, edge_dst, conductance, w_in_h, w_in_m, bias_in, w_out, ln_gain, ln_shift, w_read):
    quota = BLK_DEV // REGIONS
    dest_idx = jnp.arange(REGIONS, dtype=jnp.int32)[:, None, None]
    src_idx = jnp.arange(REGIONS, dtype=jnp.int32)[None, :, None]
    dest_block = dest_idx * BLK_DEV + recv_slot.reshape(REGIONS, REGIONS, quota)
    sent = jnp.transpose(send_order.reshape(REGIONS, REGIONS, quota), (1, 0, 2))
    src_block = src_idx * BLK_DEV + sent
    source_of = jnp.zeros((BLOCKS,), jnp.int32).at[dest_block.reshape(-1)].set(src_block.reshape(-1).astype(jnp.int32))
    blocked = enc_feat.reshape(WIDTH, BLOCKS, BLOCK)
    state = blocked[:, source_of, :].reshape(WIDTH, NODES)
    table = neighbour_blocks(want, neighbours)
    rows = jnp.arange(BLOCKS, dtype=jnp.int32)
    for layer_id in range(LAYERS):
        message = jnp.zeros((WIDTH, NODES), jnp.float32)
        for column in range(NBR):
            source_cols = (table[:, column][:, None] * BLOCK + edge_src[:, column, :]).reshape(-1)
            target_cols = (rows[:, None] * BLOCK + edge_dst[:, column, :]).reshape(-1)
            weights = conductance[:, column, :].reshape(-1).astype(jnp.float32)
            values = state[:, source_cols].astype(jnp.float32) * weights[None, :]
            message = message.at[:, target_cols].add(values)
        message = message.astype(jnp.bfloat16)
        pre = jnp.dot(w_in_h[layer_id], state, preferred_element_type=jnp.float32)
        pre = pre + jnp.dot(w_in_m[layer_id], message, preferred_element_type=jnp.float32)
        inner = jnp.maximum(pre + bias_in[layer_id][:, None], 0.0).astype(jnp.bfloat16)
        result = jnp.dot(w_out[layer_id], inner, preferred_element_type=jnp.float32)
        center = lax.optimization_barrier(jnp.mean(result, axis=0, keepdims=True))
        spread = lax.optimization_barrier(jnp.mean((result - center) ** 2, axis=0, keepdims=True))
        normed = (result - center) * lax.rsqrt(spread + 1e-05)
        update = normed * ln_gain[layer_id][:, None] + ln_shift[layer_id][:, None]
        state = (state.astype(jnp.float32) + update).astype(jnp.bfloat16)
    pressure = lax.optimization_barrier(jnp.sum(w_read[:, None] * state.astype(jnp.float32), axis=0))
    return (state, pressure)
```

```python
import functools

import jax
import jax.numpy as jnp
from jax import lax
from jax.experimental import pallas as pl
from jax.experimental.pallas import tpu as pltpu
from jax.sharding import PartitionSpec as P

BLOCK = 128
NBR = 8
CAPACITY = 4
LAYERS = 2
MESH = pl.DeviceIdType.MESH
NT = (((1,), (1,)), ((), ()))


def wait_bytes(ref, sem):
    pltpu.make_async_copy(ref, ref, sem).wait()


def network_kernel(
    send_order, slot_of, neighbours, want_row, enc_hbm, src_hbm, dst_hbm, cond_hbm,
    w_in_h, w_in_m, w_out, bias_in, ln_gain, ln_shift, w_read,
    hidden, pressure,
    enc, edge_src, edge_dst, cond, enc_stage, enc_in, want_in, want_smem,
    state0, ext0, ext1, halo0, halo1, tiles, message0, message1, x0, x1, renewed,
    exports1, others1, final, press_stage, press_in,
    w_stage, w_all, v_rows, v_stage, v_all, w_out_all,
    local_sem, send_sem, recv_sem,
):
    regions = lax.axis_size("region")
    feats = lax.axis_size("feat")
    me = lax.axis_index("region")
    my_feat = lax.axis_index("feat")
    blocks = neighbours.shape[0]
    exports = blocks // 2
    rows = enc.shape[1]
    width = rows * feats
    half = blocks // feats // 2

    loads_enc = [
        pltpu.make_async_copy(
            enc_hbm.at[:, block * BLOCK : (block + 1) * BLOCK], enc.at[block], local_sem.at[0]
        )
        for block in range(neighbours.shape[0])
    ]
    load_src = pltpu.make_async_copy(src_hbm, edge_src, local_sem.at[1])
    load_dst = pltpu.make_async_copy(dst_hbm, edge_dst, local_sem.at[2])
    load_cond = pltpu.make_async_copy(cond_hbm, cond, local_sem.at[3])
    for load in (*loads_enc, load_src, load_dst, load_cond):
        load.start()

    def region_peer(step):
        return lax.rem(me + step, regions)

    def feat_peer(step):
        return lax.rem(my_feat + step, feats)

    barrier = pltpu.get_barrier_semaphore()

    @pl.loop(1, regions)
    def _(step):
        pl.semaphore_signal(barrier, inc=1, device_id=(region_peer(step), my_feat), device_id_type=MESH)

    @pl.loop(1, feats)
    def _(step):
        pl.semaphore_signal(barrier, inc=1, device_id=(me, feat_peer(step)), device_id_type=MESH)

    eye = (
        lax.broadcasted_iota(jnp.int32, (rows, rows), 0)
        == lax.broadcasted_iota(jnp.int32, (rows, rows), 1)
    )
    mine = pl.ds(pl.multiple_of(my_feat * rows, rows), rows)
    for layer in range(LAYERS):
        w_stage[layer, :, 0:width] = w_in_h[layer]
        w_stage[layer, :, width : 2 * width] = w_in_m[layer]
        w_stage[layer, :, 2 * width :] = lax.dot_general(
            eye.astype(jnp.bfloat16), w_out[layer], NT, preferred_element_type=jnp.float32
        ).astype(jnp.bfloat16)
        w_all[layer, mine, :] = w_stage[layer]
    v_rows[...] = jnp.zeros_like(v_rows)
    v_rows[0:2, :] = bias_in[...]
    v_rows[2:4, :] = ln_gain[...]
    v_rows[4:6, :] = ln_shift[...]
    v_rows[6:7, :] = w_read[...]
    v_stage[...] = jnp.zeros_like(v_stage)
    v_stage[:, 0:8] = lax.dot_general(
        eye.astype(jnp.float32), v_rows[...], NT,
        precision=lax.Precision.HIGHEST, preferred_element_type=jnp.float32,
    )
    v_all[mine, :] = v_stage[...]
    want_in[me] = want_row[...]

    wait_bytes(enc, local_sem.at[0])

    @pl.loop(0, regions)
    def _(step):
        enc_stage[step] = enc[send_order[0, region_peer(step)]]

    enc_in[me] = enc_stage[0]

    pl.semaphore_wait(barrier, regions + feats - 2)

    @pl.loop(1, regions)
    def _(step):
        pltpu.make_async_remote_copy(
            enc_stage.at[step], enc_in.at[me], send_sem.at[0], recv_sem.at[0],
            device_id=(region_peer(step), my_feat), device_id_type=MESH,
        ).start()

    @pl.loop(1, regions)
    def _(step):
        pltpu.make_async_remote_copy(
            want_row, want_in.at[me], send_sem.at[1], recv_sem.at[1],
            device_id=(region_peer(step), my_feat), device_id_type=MESH,
        ).start()

    @pl.loop(1, feats)
    def _(step):
        peer = (me, feat_peer(step))
        pltpu.make_async_remote_copy(
            w_stage, w_all.at[:, mine, :], send_sem.at[2], recv_sem.at[2],
            device_id=peer, device_id_type=MESH,
        ).start()
        pltpu.make_async_remote_copy(
            v_stage, v_all.at[mine, :], send_sem.at[3], recv_sem.at[3],
            device_id=peer, device_id_type=MESH,
        ).start()

    load_src.wait()
    load_dst.wait()
    load_cond.wait()

    def build_tiles(block):
        pores = lax.broadcasted_iota(jnp.int32, (BLOCK, BLOCK), 0)
        for column in range(NBR):
            src = edge_src[block, column : column + 1, :]
            dst = edge_dst[block, column : column + 1, :]
            weight = cond[block, column : column + 1, :].astype(jnp.float32)
            src_hot = jnp.where(pores == src, 1.0, 0.0).astype(jnp.bfloat16)
            dst_hot = jnp.where(pores == dst, weight, 0.0).astype(jnp.bfloat16)
            tiles[block, column * BLOCK : (column + 1) * BLOCK, :] = lax.dot_general(
                src_hot, dst_hot, NT, preferred_element_type=jnp.float32
            ).astype(jnp.bfloat16)

    early = blocks // 4

    @pl.loop(0, early)
    def _(block):
        build_tiles(block)

    wait_bytes(enc_in.at[pl.ds(0, regions - 1)], recv_sem.at[0])

    @pl.loop(0, blocks)
    def _(slot):
        value = enc_in[slot_of[0, slot]]
        state0[slot] = value
        ext0[slot] = value

    wait_bytes(want_in.at[pl.ds(0, regions - 1)], recv_sem.at[1])
    to_smem = pltpu.make_async_copy(want_in, want_smem, local_sem.at[4])
    to_smem.start()
    to_smem.wait()

    def stage_halo(step, source, first, halo):
        region = region_peer(step)
        for panel in range(CAPACITY):
            entry = want_smem[region, 0, me * CAPACITY + panel]
            halo[step, panel] = source[first + entry]

    def send_halo(step, halo, ext, index):
        pltpu.make_async_remote_copy(
            halo.at[step], ext.at[pl.ds(blocks + me * CAPACITY, CAPACITY)],
            send_sem.at[index], recv_sem.at[index],
            device_id=(region_peer(step), my_feat), device_id_type=MESH,
        ).start()

    def exchange_halo(source, first, halo, ext, index):
        @pl.loop(1, regions)
        def _(step):
            stage_halo(step, source, first, halo)
            send_halo(step, halo, ext, index)

        stage_halo(0, source, first, halo)
        for panel in range(CAPACITY):
            ext[blocks + me * CAPACITY + panel] = halo[0, panel]

    exchange_halo(state0, exports, halo0, ext0, 4)

    def share(side):
        def from_peer(step):
            return pl.ds(side * exports + feat_peer(step) * half, half)

        return from_peer

    def to_owner(source, x, side, first_row, index):
        into = pl.ds(pl.multiple_of(first_row + my_feat * rows, rows), rows)
        where = share(side)

        @pl.loop(1, feats)
        def _(step):
            pltpu.make_async_remote_copy(
                source.at[where(step)], x.at[side, :, into, :],
                send_sem.at[index], recv_sem.at[index],
                device_id=(me, feat_peer(step)), device_id_type=MESH,
            ).start()

        x[side, :, into, :] = source[where(0)]

    to_owner(state0, x0, 1, 0, 5)
    to_owner(state0, x0, 0, 0, 6)

    @pl.loop(early, blocks)
    def _(block):
        build_tiles(block)

    wait_bytes(w_all.at[:, pl.ds(0, width - rows), :], recv_sem.at[2])
    wait_bytes(v_all.at[pl.ds(0, width - rows), :], recv_sem.at[3])
    eye_all = (
        lax.broadcasted_iota(jnp.int32, (width, width), 0)
        == lax.broadcasted_iota(jnp.int32, (width, width), 1)
    ).astype(jnp.bfloat16)
    for layer in range(LAYERS):
        w_out_all[layer] = lax.dot_general(
            eye_all, w_all[layer, :, 2 * width :], NT, preferred_element_type=jnp.float32
        ).astype(jnp.bfloat16)

    def aggregate(ext, message, side):
        @pl.loop(side * exports, (side + 1) * exports)
        def _(block):
            sources = jnp.concatenate(
                [ext[neighbours[block, column]] for column in range(NBR)], axis=1
            )
            message[block] = jnp.dot(
                sources, tiles[block], preferred_element_type=jnp.float32
            ).astype(jnp.bfloat16)

    def update(x, side, layer):
        both = jnp.concatenate([x[side, j] for j in range(half)], axis=1)
        vectors = v_all[...]
        pre = jnp.dot(w_all[layer, :, 0 : 2 * width], both, preferred_element_type=jnp.float32)
        inner = jnp.maximum(pre + vectors[:, layer : layer + 1], 0.0).astype(jnp.bfloat16)
        y = jnp.dot(w_out_all[layer], inner, preferred_element_type=jnp.float32)
        mean = jnp.mean(y, axis=0, keepdims=True)
        shifted = y - mean
        var = jnp.mean(shifted * shifted, axis=0, keepdims=True)
        normed = shifted * lax.rsqrt(var + 1e-05)
        change = normed * vectors[:, 2 + layer : 3 + layer] + vectors[:, 4 + layer : 5 + layer]
        return (both[0:width].astype(jnp.float32) + change).astype(jnp.bfloat16)

    def wait_owner(x, side, index):
        wait_bytes(x.at[side, :, pl.ds(0, width - rows), :], recv_sem.at[index])

    def give_back(x, into, side, first, index):
        where = pl.ds(first + my_feat * half, half)

        def part(step):
            return x.at[side, :, pl.ds(pl.multiple_of(feat_peer(step) * rows, rows), rows), :]

        @pl.loop(1, feats)
        def _(step):
            pltpu.make_async_remote_copy(
                part(step), into.at[where], send_sem.at[index], recv_sem.at[index],
                device_id=(me, feat_peer(step)), device_id_type=MESH,
            ).start()

        into[where] = part(0)[...]

    def wait_back(into, index):
        wait_bytes(into.at[pl.ds(0, half * (feats - 1))], recv_sem.at[index])

    halo_bytes = pl.ds(0, (regions - 1) * CAPACITY)
    wait_bytes(ext0.at[halo_bytes], recv_sem.at[4])
    for side in (1, 0):
        aggregate(ext0, message0, side)
        to_owner(message0, x0, side, width, 8 - side)
    for side, into in ((1, exports1), (0, others1)):
        wait_owner(x0, side, 6 - side)
        wait_owner(x0, side, 8 - side)
        new = update(x0, side, 0)
        for j in range(half):
            x1[side, j, 0:width, :] = new[:, j * BLOCK : (j + 1) * BLOCK]
        give_back(x1, into, side, 0, 10 - side)

    wait_back(exports1, 9)
    exchange_halo(exports1, 0, halo1, ext1, 11)
    ext1[pl.ds(exports, exports)] = exports1[...]
    wait_back(others1, 10)
    ext1[pl.ds(0, exports)] = others1[...]
    wait_bytes(ext1.at[halo_bytes], recv_sem.at[11])
    for side in (1, 0):
        aggregate(ext1, message1, side)
        to_owner(message1, x1, side, width, 13 - side)
    for side in (1, 0):
        wait_owner(x1, side, 13 - side)
        new = update(x1, side, 1)
        scaled = v_all[:, 6:7] * new.astype(jnp.float32)
        total = jnp.sum(scaled, axis=0, keepdims=True)
        for j in range(half):
            renewed[side, j] = new[:, j * BLOCK : (j + 1) * BLOCK]
            press_stage[0, side * half + j : side * half + j + 1, :] = (
                total[:, j * BLOCK : (j + 1) * BLOCK]
            )
        give_back(renewed, final, side, side * exports, 15 - side)

    @pl.loop(1, feats)
    def _(step):
        pltpu.make_async_remote_copy(
            press_stage, press_in.at[pl.ds(my_feat, 1)], send_sem.at[16], recv_sem.at[16],
            device_id=(me, feat_peer(step)), device_id_type=MESH,
        ).start()

    press_in[pl.ds(my_feat, 1)] = press_stage[...]
    wait_back(final, 14)
    wait_back(final, 15)
    for block in range(blocks):
        hidden[:, block * BLOCK : (block + 1) * BLOCK] = final[block]
    wait_bytes(press_in.at[pl.ds(0, feats - 1)], recv_sem.at[16])
    for feat in range(feats):
        for side in range(2):
            first = side * exports + feat * half
            pressure[first : first + half, :] = press_in[feat, side * half : (side + 1) * half, :]

    wait_bytes(enc_stage.at[pl.ds(1, regions - 1)], send_sem.at[0])
    wait_bytes(want_in.at[pl.ds(0, regions - 1)], send_sem.at[1])
    wait_bytes(w_all.at[:, pl.ds(0, width - rows), :], send_sem.at[2])
    wait_bytes(v_all.at[pl.ds(0, width - rows), :], send_sem.at[3])
    wait_bytes(halo0.at[pl.ds(1, regions - 1)], send_sem.at[4])
    wait_bytes(halo1.at[pl.ds(1, regions - 1)], send_sem.at[11])
    for index in (5, 6, 7, 8, 9, 10, 12, 13, 14, 15):
        wait_bytes(state0.at[pl.ds(0, half * (feats - 1))], send_sem.at[index])
    wait_bytes(press_in.at[pl.ds(0, feats - 1)], send_sem.at[16])


def on_device(
    enc_feat, send_order, recv_slot, want, neighbours, edge_src, edge_dst, conductance,
    w_in_h, w_in_m, bias_in, w_out, ln_gain, ln_shift, w_read,
):
    regions = lax.axis_size("region")
    feats = lax.axis_size("feat")
    rows, nodes = enc_feat.shape
    blocks = neighbours.shape[0]
    exports = blocks // 2
    width = rows * feats
    own = blocks // feats
    half = own // 2
    panels = regions * CAPACITY
    bf16, f32, i32 = jnp.bfloat16, jnp.float32, jnp.int32
    slots = jnp.arange(blocks, dtype=i32)
    slot_of = jnp.sum(
        jnp.where(recv_slot == slots[:, None], slots[None, :], 0), axis=1, dtype=i32
    ).reshape(1, blocks)
    want_row = jnp.pad(want.reshape(1, panels), ((0, 0), (0, BLOCK - panels)))
    smem = pl.BlockSpec(memory_space=pltpu.SMEM)
    vmem = pl.BlockSpec(memory_space=pltpu.VMEM)
    hbm = pl.BlockSpec(memory_space=pl.ANY)
    phases = 17
    hidden, pressure = pl.pallas_call(
        network_kernel,
        out_shape=(
            jax.ShapeDtypeStruct((rows, nodes), bf16),
            jax.ShapeDtypeStruct((blocks, BLOCK), f32),
        ),
        in_specs=[smem, smem, smem, vmem, hbm, hbm, hbm, hbm] + [vmem] * 7,
        out_specs=(vmem, vmem),
        scratch_shapes=[
            pltpu.VMEM((blocks, rows, BLOCK), bf16),
            pltpu.VMEM((blocks, NBR, BLOCK), i32),
            pltpu.VMEM((blocks, NBR, BLOCK), i32),
            pltpu.VMEM((blocks, NBR, BLOCK), bf16),
            pltpu.VMEM((regions, rows, BLOCK), bf16),
            pltpu.VMEM((regions, rows, BLOCK), bf16),
            pltpu.VMEM((regions, 1, BLOCK), i32),
            pltpu.SMEM((regions, 1, BLOCK), i32),
            pltpu.VMEM((blocks, rows, BLOCK), bf16),
            pltpu.VMEM((blocks + panels, rows, BLOCK), bf16),
            pltpu.VMEM((blocks + panels, rows, BLOCK), bf16),
            pltpu.VMEM((regions, CAPACITY, rows, BLOCK), bf16),
            pltpu.VMEM((regions, CAPACITY, rows, BLOCK), bf16),
            pltpu.VMEM((blocks, NBR * BLOCK, BLOCK), bf16),
            pltpu.VMEM((blocks, rows, BLOCK), bf16),
            pltpu.VMEM((blocks, rows, BLOCK), bf16),
            pltpu.VMEM((2, half, 2 * width, BLOCK), bf16),
            pltpu.VMEM((2, half, 2 * width, BLOCK), bf16),
            pltpu.VMEM((2, half, width, BLOCK), bf16),
            pltpu.VMEM((exports, rows, BLOCK), bf16),
            pltpu.VMEM((exports, rows, BLOCK), bf16),
            pltpu.VMEM((blocks, rows, BLOCK), bf16),
            pltpu.VMEM((1, own, BLOCK), f32),
            pltpu.VMEM((feats, own, BLOCK), f32),
            pltpu.VMEM((LAYERS, rows, 3 * width), bf16),
            pltpu.VMEM((LAYERS, width, 3 * width), bf16),
            pltpu.VMEM((8, rows), f32),
            pltpu.VMEM((rows, BLOCK), f32),
            pltpu.VMEM((width, BLOCK), f32),
            pltpu.VMEM((LAYERS, width, width), bf16),
            pltpu.SemaphoreType.DMA((5,)),
            pltpu.SemaphoreType.DMA((phases,)),
            pltpu.SemaphoreType.DMA((phases,)),
        ],
        compiler_params=pltpu.CompilerParams(
            collective_id=0, has_side_effects=True, vmem_limit_bytes=40 * 1024 * 1024
        ),
        cost_estimate=pl.CostEstimate(
            flops=2 * blocks * NBR * BLOCK * BLOCK * (BLOCK + 2 * rows),
            bytes_accessed=2**20, transcendentals=0,
        ),
    )(
        send_order, slot_of, neighbours, want_row, enc_feat, edge_src, edge_dst, conductance,
        w_in_h, w_in_m, w_out, bias_in, ln_gain, ln_shift, w_read.reshape(1, rows),
    )
    return hidden, pressure.reshape(nodes)


def solution(mesh):
    return jax.shard_map(
        on_device,
        mesh=mesh,
        in_specs=(
            P("feat", "region"),
            P("region", None),
            P("region", None),
            P("region", None, None),
            P("region", None),
            P("region", None, None),
            P("region", None, None),
            P("region", None, None),
            P(None, "feat", None),
            P(None, "feat", None),
            P(None, "feat"),
            P(None, None, "feat"),
            P(None, "feat"),
            P(None, "feat"),
            P("feat"),
        ),
        out_specs=(P("feat", "region"), P("region")),
        check_vma=False,
    )
```

```python
import functools

import jax
import jax.numpy as jnp
from jax import lax
from jax.experimental import pallas as pl
from jax.experimental.pallas import tpu as pltpu
from jax.sharding import PartitionSpec as P

BLOCK = 128
NBR = 8
CAPACITY = 4
LAYERS = 2
MESH = pl.DeviceIdType.MESH
NT = (((1,), (1,)), ((), ()))


def wait_bytes(ref, sem):
    pltpu.make_async_copy(ref, ref, sem).wait()


def network_kernel(
    order_hbm, slot_hbm, nbr_hbm, want_hbm, enc_hbm, src_hbm, dst_hbm, cond_hbm,
    w_in_h_hbm, w_in_m_hbm, w_out_hbm, bias_hbm, gain_hbm, shift_hbm, read_hbm,
    hidden, pressure,
    send_order, recv_slot, neighbours, want_row, inverse, slot_of,
    w_in_h, w_in_m, w_out, bias_in, ln_gain, ln_shift, w_read,
    enc, edge_src, edge_dst, cond, enc_stage, enc_in, want_in, want_smem,
    state0, ext0, ext1, halo0, halo1, tiles, message0, message1, x0, x1, renewed,
    exports1, others1, final, press_stage, press_in,
    w_stage, w_all, v_rows, v_stage, v_all, w_out_all,
    local_sem, send_sem, recv_sem,
):
    regions = lax.axis_size("region")
    feats = lax.axis_size("feat")
    me = lax.axis_index("region")
    my_feat = lax.axis_index("feat")
    blocks = enc.shape[0]
    exports = blocks // 2
    rows = enc.shape[1]
    width = rows * feats
    half = blocks // feats // 2

    sent = []

    def drain():
        for ref, index in sent:
            wait_bytes(ref, send_sem.at[index])

    loads_enc = [
        pltpu.make_async_copy(
            enc_hbm.at[:, block * BLOCK : (block + 1) * BLOCK], enc.at[block], local_sem.at[0]
        )
        for block in range(blocks)
    ]
    small = (
        (order_hbm, send_order), (slot_hbm, recv_slot), (want_hbm, want_row),
        (w_in_h_hbm, w_in_h), (w_in_m_hbm, w_in_m), (w_out_hbm, w_out), (bias_hbm, bias_in),
        (gain_hbm, ln_gain), (shift_hbm, ln_shift), (read_hbm, w_read),
        (src_hbm, edge_src), (dst_hbm, edge_dst), (cond_hbm, cond), (nbr_hbm, neighbours),
    )
    loads = [
        pltpu.make_async_copy(source, target, local_sem.at[1 + at])
        for at, (source, target) in enumerate(small)
    ]
    for load in (*loads[:2], *loads_enc, *loads[2:]):
        load.start()

    def region_peer(step):
        return lax.rem(me + step, regions)

    def feat_peer(step):
        return lax.rem(my_feat + step, feats)

    barrier = pltpu.get_barrier_semaphore()

    @pl.loop(1, regions)
    def _(step):
        pl.semaphore_signal(barrier, inc=1, device_id=(region_peer(step), my_feat), device_id_type=MESH)

    @pl.loop(1, feats)
    def _(step):
        pl.semaphore_signal(barrier, inc=1, device_id=(me, feat_peer(step)), device_id_type=MESH)

    loads[0].wait()
    loads[1].wait()
    wait_bytes(enc, local_sem.at[0])

    @pl.loop(0, regions)
    def _(step):
        enc_stage[step] = enc[send_order[0, region_peer(step)]]

    enc_in[me] = enc_stage[0]

    for load in loads[2:10]:
        load.wait()
    eye = (
        lax.broadcasted_iota(jnp.int32, (rows, rows), 0)
        == lax.broadcasted_iota(jnp.int32, (rows, rows), 1)
    )
    mine = pl.ds(pl.multiple_of(my_feat * rows, rows), rows)
    for layer in range(LAYERS):
        w_stage[layer, :, 0:width] = w_in_h[layer]
        w_stage[layer, :, width : 2 * width] = w_in_m[layer]
        w_stage[layer, :, 2 * width :] = w_out[layer]
        w_all[layer, mine, :] = w_stage[layer]
    v_rows[...] = jnp.zeros_like(v_rows)
    v_rows[0:2, :] = bias_in[...]
    v_rows[2:4, :] = ln_gain[...]
    v_rows[4:6, :] = ln_shift[...]
    v_rows[6:7, :] = w_read[...]
    v_stage[...] = jnp.zeros_like(v_stage)
    v_stage[:, 0:8] = lax.dot_general(
        eye.astype(jnp.float32), v_rows[...], NT,
        precision=lax.Precision.HIGHEST, preferred_element_type=jnp.float32,
    )
    v_all[mine, :] = v_stage[...]
    want_in[me] = want_row[...]

    slots = lax.broadcasted_iota(jnp.int32, inverse.shape, 1)
    found = jnp.zeros(inverse.shape, jnp.int32)
    for source in range(regions):
        found = jnp.where(slots == recv_slot[0, source], source, found)
    inverse[...] = found
    load_slots = pltpu.make_async_copy(inverse, slot_of, local_sem.at[16])
    load_slots.start()

    pl.semaphore_wait(barrier, regions + feats - 2)

    @pl.loop(1, regions)
    def _(step):
        pltpu.make_async_remote_copy(
            enc_stage.at[step], enc_in.at[me], send_sem.at[0], recv_sem.at[0],
            device_id=(region_peer(step), my_feat), device_id_type=MESH,
        ).start()

    @pl.loop(1, regions)
    def _(step):
        pltpu.make_async_remote_copy(
            want_row, want_in.at[me], send_sem.at[1], recv_sem.at[1],
            device_id=(region_peer(step), my_feat), device_id_type=MESH,
        ).start()

    @pl.loop(1, feats)
    def _(step):
        peer = (me, feat_peer(step))
        pltpu.make_async_remote_copy(
            w_stage, w_all.at[:, mine, :], send_sem.at[2], recv_sem.at[2],
            device_id=peer, device_id_type=MESH,
        ).start()
        pltpu.make_async_remote_copy(
            v_stage, v_all.at[mine, :], send_sem.at[3], recv_sem.at[3],
            device_id=peer, device_id_type=MESH,
        ).start()

    sent.append((enc_stage.at[pl.ds(1, regions - 1)], 0))
    sent.append((want_in.at[pl.ds(0, regions - 1)], 1))
    sent.append((w_all.at[:, pl.ds(0, width - rows), :], 2))
    sent.append((v_all.at[pl.ds(0, width - rows), :], 3))

    for load in loads[10:]:
        load.wait()

    def build_tiles(block):
        pores = lax.broadcasted_iota(jnp.int32, (BLOCK, BLOCK), 0)
        for column in range(NBR):
            src = edge_src[block, column : column + 1, :]
            dst = edge_dst[block, column : column + 1, :]
            weight = cond[block, column : column + 1, :].astype(jnp.float32)
            src_hot = jnp.where(pores == src, 1.0, 0.0).astype(jnp.bfloat16)
            dst_hot = jnp.where(pores == dst, weight, 0.0).astype(jnp.bfloat16)
            tiles[block, column * BLOCK : (column + 1) * BLOCK, :] = lax.dot_general(
                src_hot, dst_hot, NT, preferred_element_type=jnp.float32
            ).astype(jnp.bfloat16)

    early = blocks // 4

    @pl.loop(0, early)
    def _(block):
        build_tiles(block)

    wait_bytes(enc_in.at[pl.ds(0, regions - 1)], recv_sem.at[0])

    load_slots.wait()

    @pl.loop(0, blocks)
    def _(slot):
        value = enc_in[slot_of[0, slot]]
        state0[slot] = value
        ext0[slot] = value

    wait_bytes(want_in.at[pl.ds(0, regions - 1)], recv_sem.at[1])
    to_smem = pltpu.make_async_copy(want_in, want_smem, local_sem.at[15])
    to_smem.start()
    to_smem.wait()

    def stage_halo(step, source, first, halo):
        region = region_peer(step)
        for panel in range(CAPACITY):
            entry = want_smem[region, panel, me]
            halo[step, panel] = source[first + entry]

    def send_halo(step, halo, ext, index):
        pltpu.make_async_remote_copy(
            halo.at[step], ext.at[pl.ds(blocks + me * CAPACITY, CAPACITY)],
            send_sem.at[index], recv_sem.at[index],
            device_id=(region_peer(step), my_feat), device_id_type=MESH,
        ).start()

    def exchange_halo(source, first, halo, ext, index):
        @pl.loop(1, regions)
        def _(step):
            stage_halo(step, source, first, halo)
            send_halo(step, halo, ext, index)

        sent.append((halo.at[pl.ds(1, regions - 1)], index))
        stage_halo(0, source, first, halo)
        for panel in range(CAPACITY):
            ext[blocks + me * CAPACITY + panel] = halo[0, panel]

    exchange_halo(state0, exports, halo0, ext0, 4)

    def share(side):
        def from_peer(step):
            return pl.ds(side * exports + feat_peer(step) * half, half)

        return from_peer

    def to_owner(source, x, side, first_row, index):
        into = pl.ds(pl.multiple_of(first_row + my_feat * rows, rows), rows)
        where = share(side)

        @pl.loop(1, feats)
        def _(step):
            pltpu.make_async_remote_copy(
                source.at[where(step)], x.at[side, :, into, :],
                send_sem.at[index], recv_sem.at[index],
                device_id=(me, feat_peer(step)), device_id_type=MESH,
            ).start()

        sent.append((state0.at[pl.ds(0, half * (feats - 1))], index))
        x[side, :, into, :] = source[where(0)]

    to_owner(state0, x0, 1, 0, 5)
    to_owner(state0, x0, 0, 0, 6)

    @pl.loop(early, blocks)
    def _(block):
        build_tiles(block)

    wait_bytes(w_all.at[:, pl.ds(0, width - rows), :], recv_sem.at[2])
    wait_bytes(v_all.at[pl.ds(0, width - rows), :], recv_sem.at[3])
    eye_all = (
        lax.broadcasted_iota(jnp.int32, (width, width), 0)
        == lax.broadcasted_iota(jnp.int32, (width, width), 1)
    ).astype(jnp.bfloat16)
    for layer in range(LAYERS):
        w_out_all[layer] = lax.dot_general(
            eye_all, w_all[layer, :, 2 * width :], NT, preferred_element_type=jnp.float32
        ).astype(jnp.bfloat16)

    def aggregate(ext, message, side):
        @pl.loop(side * exports, (side + 1) * exports)
        def _(block):
            sources = jnp.concatenate(
                [ext[neighbours[column, block]] for column in range(NBR)], axis=1
            )
            message[block] = jnp.dot(
                sources, tiles[block], preferred_element_type=jnp.float32
            ).astype(jnp.bfloat16)

    def update(x, side, layer):
        both = jnp.concatenate([x[side, j] for j in range(half)], axis=1)
        vectors = v_all[...]
        pre = jnp.dot(w_all[layer, :, 0 : 2 * width], both, preferred_element_type=jnp.float32)
        inner = jnp.maximum(pre + vectors[:, layer : layer + 1], 0.0).astype(jnp.bfloat16)
        y = jnp.dot(w_out_all[layer], inner, preferred_element_type=jnp.float32)
        mean = jnp.mean(y, axis=0, keepdims=True)
        shifted = y - mean
        var = jnp.mean(shifted * shifted, axis=0, keepdims=True)
        normed = shifted * lax.rsqrt(var + 1e-05)
        change = normed * vectors[:, 2 + layer : 3 + layer] + vectors[:, 4 + layer : 5 + layer]
        return (both[0:width].astype(jnp.float32) + change).astype(jnp.bfloat16)

    def wait_owner(x, side, index):
        wait_bytes(x.at[side, :, pl.ds(0, width - rows), :], recv_sem.at[index])

    def give_back(x, into, side, first, index):
        where = pl.ds(first + my_feat * half, half)

        def part(step):
            return x.at[side, :, pl.ds(pl.multiple_of(feat_peer(step) * rows, rows), rows), :]

        @pl.loop(1, feats)
        def _(step):
            pltpu.make_async_remote_copy(
                part(step), into.at[where], send_sem.at[index], recv_sem.at[index],
                device_id=(me, feat_peer(step)), device_id_type=MESH,
            ).start()

        sent.append((state0.at[pl.ds(0, half * (feats - 1))], index))
        into[where] = part(0)[...]

    def wait_back(into, index):
        wait_bytes(into.at[pl.ds(0, half * (feats - 1))], recv_sem.at[index])

    halo_bytes = pl.ds(0, (regions - 1) * CAPACITY)
    wait_bytes(ext0.at[halo_bytes], recv_sem.at[4])
    for side in (1, 0):
        aggregate(ext0, message0, side)
        to_owner(message0, x0, side, width, 8 - side)
    for side, into in ((1, exports1), (0, others1)):
        wait_owner(x0, side, 6 - side)
        wait_owner(x0, side, 8 - side)
        new = update(x0, side, 0)
        for j in range(half):
            x1[side, j, 0:width, :] = new[:, j * BLOCK : (j + 1) * BLOCK]
        give_back(x1, into, side, 0, 10 - side)

    wait_back(exports1, 9)
    exchange_halo(exports1, 0, halo1, ext1, 11)
    ext1[pl.ds(exports, exports)] = exports1[...]
    wait_back(others1, 10)
    ext1[pl.ds(0, exports)] = others1[...]
    wait_bytes(ext1.at[halo_bytes], recv_sem.at[11])
    for side in (1, 0):
        aggregate(ext1, message1, side)
        to_owner(message1, x1, side, width, 13 - side)
    for side in (1, 0):
        wait_owner(x1, side, 13 - side)
        new = update(x1, side, 1)
        scaled = v_all[:, 6:7] * new.astype(jnp.float32)
        total = jnp.sum(scaled, axis=0, keepdims=True)
        for j in range(half):
            renewed[side, j] = new[:, j * BLOCK : (j + 1) * BLOCK]
            press_stage[0, side * half + j : side * half + j + 1, :] = (
                total[:, j * BLOCK : (j + 1) * BLOCK]
            )
        give_back(renewed, final, side, side * exports, 15 - side)

    @pl.loop(1, feats)
    def _(step):
        pltpu.make_async_remote_copy(
            press_stage, press_in.at[pl.ds(my_feat, 1)], send_sem.at[16], recv_sem.at[16],
            device_id=(me, feat_peer(step)), device_id_type=MESH,
        ).start()

    sent.append((press_in.at[pl.ds(0, feats - 1)], 16))
    press_in[pl.ds(my_feat, 1)] = press_stage[...]
    wait_back(final, 14)
    wait_back(final, 15)
    for block in range(blocks):
        hidden[:, block * BLOCK : (block + 1) * BLOCK] = final[block]
    wait_bytes(press_in.at[pl.ds(0, feats - 1)], recv_sem.at[16])
    for feat in range(feats):
        for side in range(2):
            first = side * exports + feat * half
            pressure[first : first + half, :] = press_in[feat, side * half : (side + 1) * half, :]

    drain()


def on_device(
    enc_feat, send_order, recv_slot, want, neighbours, edge_src, edge_dst, conductance,
    w_in_h, w_in_m, bias_in, w_out, ln_gain, ln_shift, w_read,
):
    regions = lax.axis_size("region")
    feats = lax.axis_size("feat")
    rows, nodes = enc_feat.shape
    blocks = neighbours.shape[0]
    exports = blocks // 2
    width = rows * feats
    own = blocks // feats
    half = own // 2
    panels = regions * CAPACITY
    bf16, f32, i32 = jnp.bfloat16, jnp.float32, jnp.int32
    vmem = pl.BlockSpec(memory_space=pltpu.VMEM)
    hbm = pl.BlockSpec(memory_space=pl.ANY)
    phases = 17
    hidden, pressure = pl.pallas_call(
        network_kernel,
        out_shape=(
            jax.ShapeDtypeStruct((rows, nodes), bf16),
            jax.ShapeDtypeStruct((blocks, BLOCK), f32),
        ),
        in_specs=[hbm] * 15,
        out_specs=(vmem, vmem),
        scratch_shapes=[
            pltpu.SMEM((1, blocks), i32),
            pltpu.SMEM((1, regions), i32),
            pltpu.SMEM((NBR, blocks), i32),
            pltpu.VMEM((CAPACITY, regions), i32),
            pltpu.VMEM((1, BLOCK), i32),
            pltpu.SMEM((1, BLOCK), i32),
            pltpu.VMEM((LAYERS, rows, width), bf16),
            pltpu.VMEM((LAYERS, rows, width), bf16),
            pltpu.VMEM((LAYERS, rows, width), bf16),
            pltpu.VMEM((LAYERS, rows), f32),
            pltpu.VMEM((LAYERS, rows), f32),
            pltpu.VMEM((LAYERS, rows), f32),
            pltpu.VMEM((1, rows), f32),
            pltpu.VMEM((blocks, rows, BLOCK), bf16),
            pltpu.VMEM((blocks, NBR, BLOCK), i32),
            pltpu.VMEM((blocks, NBR, BLOCK), i32),
            pltpu.VMEM((blocks, NBR, BLOCK), bf16),
            pltpu.VMEM((regions, rows, BLOCK), bf16),
            pltpu.VMEM((regions, rows, BLOCK), bf16),
            pltpu.VMEM((regions, CAPACITY, regions), i32),
            pltpu.SMEM((regions, CAPACITY, regions), i32),
            pltpu.VMEM((blocks, rows, BLOCK), bf16),
            pltpu.VMEM((blocks + panels, rows, BLOCK), bf16),
            pltpu.VMEM((blocks + panels, rows, BLOCK), bf16),
            pltpu.VMEM((regions, CAPACITY, rows, BLOCK), bf16),
            pltpu.VMEM((regions, CAPACITY, rows, BLOCK), bf16),
            pltpu.VMEM((blocks, NBR * BLOCK, BLOCK), bf16),
            pltpu.VMEM((blocks, rows, BLOCK), bf16),
            pltpu.VMEM((blocks, rows, BLOCK), bf16),
            pltpu.VMEM((2, half, 2 * width, BLOCK), bf16),
            pltpu.VMEM((2, half, 2 * width, BLOCK), bf16),
            pltpu.VMEM((2, half, width, BLOCK), bf16),
            pltpu.VMEM((exports, rows, BLOCK), bf16),
            pltpu.VMEM((exports, rows, BLOCK), bf16),
            pltpu.VMEM((blocks, rows, BLOCK), bf16),
            pltpu.VMEM((1, own, BLOCK), f32),
            pltpu.VMEM((feats, own, BLOCK), f32),
            pltpu.VMEM((LAYERS, rows, 3 * width), bf16),
            pltpu.VMEM((LAYERS, width, 3 * width), bf16),
            pltpu.VMEM((8, rows), f32),
            pltpu.VMEM((rows, BLOCK), f32),
            pltpu.VMEM((width, BLOCK), f32),
            pltpu.VMEM((LAYERS, width, width), bf16),
            pltpu.SemaphoreType.DMA((17,)),
            pltpu.SemaphoreType.DMA((phases,)),
            pltpu.SemaphoreType.DMA((phases,)),
        ],
        compiler_params=pltpu.CompilerParams(
            collective_id=0, has_side_effects=True, vmem_limit_bytes=60 * 1024 * 1024
        ),
        cost_estimate=pl.CostEstimate(
            flops=2 * blocks * NBR * BLOCK * BLOCK * (BLOCK + 2 * rows),
            bytes_accessed=2**20, transcendentals=0,
        ),
    )(
        send_order, recv_slot, neighbours.T, want.reshape(regions, CAPACITY).T, enc_feat,
        edge_src, edge_dst, conductance, w_in_h, w_in_m, jnp.swapaxes(w_out, 1, 2), bias_in, ln_gain, ln_shift, w_read.reshape(1, rows),
    )
    return hidden, pressure.reshape(nodes)


def solution(mesh):
    return jax.shard_map(
        on_device,
        mesh=mesh,
        in_specs=(
            P("feat", "region"),
            P("region", None),
            P("region", None),
            P("region", None, None),
            P("region", None),
            P("region", None, None),
            P("region", None, None),
            P("region", None, None),
            P(None, "feat", None),
            P(None, "feat", None),
            P(None, "feat"),
            P(None, None, "feat"),
            P(None, "feat"),
            P(None, "feat"),
            P("feat"),
        ),
        out_specs=(P("feat", "region"), P("region")),
        check_vma=False,
    )
```

```python
import functools

import jax
import jax.numpy as jnp
from jax import lax
from jax.experimental import pallas as pl
from jax.experimental.pallas import tpu as pltpu
from jax.sharding import PartitionSpec as P

BLOCK = 128
NBR = 8
CAPACITY = 4
LAYERS = 2
MESH = pl.DeviceIdType.MESH
NT = (((1,), (1,)), ((), ()))


def wait_bytes(ref, sem):
    pltpu.make_async_copy(ref, ref, sem).wait()


def network_kernel(
    order_hbm, slot_hbm, nbr_hbm, want_hbm, enc_hbm, src_hbm, dst_hbm, cond_hbm,
    w_in_h_hbm, w_in_m_hbm, w_out_hbm, bias_hbm, gain_hbm, shift_hbm, read_hbm,
    hidden, pressure,
    send_order, recv_slot, neighbours, want_row, want_out, inverse, slot_of,
    w_in_h, w_in_m, w_out, bias_in, ln_gain, ln_shift, w_read,
    enc, edge_src, edge_dst, cond, enc_stage, enc_in, want_in, want_smem,
    state0, ext0, ext1, halo0, halo1, tiles, message0, message1, x0, x1, renewed,
    exports1, others1, final, press_stage, press_in,
    w_stage, w_all, v_rows, v_stage, v_all, w_out_all,
    local_sem, send_sem, recv_sem,
):
    regions = lax.axis_size("region")
    feats = lax.axis_size("feat")
    me = lax.axis_index("region")
    my_feat = lax.axis_index("feat")
    blocks = enc.shape[0]
    exports = blocks // 2
    rows = enc.shape[1]
    width = rows * feats
    half = blocks // feats // 2

    sent = []

    def drain():
        for ref, index in sent:
            wait_bytes(ref, send_sem.at[index])

    loads_enc = [
        pltpu.make_async_copy(
            enc_hbm.at[:, block * BLOCK : (block + 1) * BLOCK], enc.at[block], local_sem.at[0]
        )
        for block in range(blocks)
    ]
    small = (
        (order_hbm, send_order), (slot_hbm, recv_slot), (want_hbm, want_row),
        (w_in_h_hbm, w_in_h), (w_in_m_hbm, w_in_m), (w_out_hbm, w_out), (bias_hbm, bias_in),
        (gain_hbm, ln_gain), (shift_hbm, ln_shift), (read_hbm, w_read),
        (src_hbm, edge_src), (dst_hbm, edge_dst), (cond_hbm, cond), (nbr_hbm, neighbours),
    )
    loads = [
        pltpu.make_async_copy(source, target, local_sem.at[1 + at])
        for at, (source, target) in enumerate(small)
    ]
    for load in (*loads[:2], *loads_enc, *loads[2:]):
        load.start()

    def region_peer(step):
        return lax.rem(me + step, regions)

    def feat_peer(step):
        return lax.rem(my_feat + step, feats)

    barrier = pltpu.get_barrier_semaphore()

    @pl.loop(1, regions)
    def _(step):
        pl.semaphore_signal(barrier, inc=1, device_id=(region_peer(step), my_feat), device_id_type=MESH)

    @pl.loop(1, feats)
    def _(step):
        pl.semaphore_signal(barrier, inc=1, device_id=(me, feat_peer(step)), device_id_type=MESH)

    loads[0].wait()
    loads[1].wait()
    wait_bytes(enc, local_sem.at[0])

    @pl.loop(0, regions)
    def _(step):
        enc_stage[step] = enc[send_order[0, region_peer(step)]]

    enc_in[me] = enc_stage[0]

    for load in loads[2:10]:
        load.wait()
    eye = (
        lax.broadcasted_iota(jnp.int32, (rows, rows), 0)
        == lax.broadcasted_iota(jnp.int32, (rows, rows), 1)
    )
    mine = pl.ds(pl.multiple_of(my_feat * rows, rows), rows)
    for layer in range(LAYERS):
        w_stage[layer, :, 0:width] = w_in_h[layer]
        w_stage[layer, :, width : 2 * width] = w_in_m[layer]
        w_stage[layer, :, 2 * width :] = w_out[layer]
        w_all[layer, mine, :] = w_stage[layer]
    v_rows[...] = jnp.zeros_like(v_rows)
    v_rows[0:2, :] = bias_in[...]
    v_rows[2:4, :] = ln_gain[...]
    v_rows[4:6, :] = ln_shift[...]
    v_rows[6:7, :] = w_read[...]
    v_stage[...] = jnp.zeros_like(v_stage)
    v_stage[:, 0:8] = lax.dot_general(
        eye.astype(jnp.float32), v_rows[...], NT,
        precision=lax.Precision.HIGHEST, preferred_element_type=jnp.float32,
    )
    v_all[mine, :] = v_stage[...]
    lanes = lax.broadcasted_iota(jnp.int32, (1, BLOCK), 1)

    @pl.loop(0, regions)
    def _(region):
        row = jnp.zeros((1, BLOCK), jnp.int32)
        for panel in range(CAPACITY):
            row = jnp.where(lanes == panel, want_row[panel, region], row)
        want_out[region] = row

    want_in[me] = want_out[me]

    slots = lax.broadcasted_iota(jnp.int32, inverse.shape, 1)
    found = jnp.zeros(inverse.shape, jnp.int32)
    for source in range(regions):
        found = jnp.where(slots == recv_slot[0, source], source, found)
    inverse[...] = found
    load_slots = pltpu.make_async_copy(inverse, slot_of, local_sem.at[16])
    load_slots.start()

    pl.semaphore_wait(barrier, regions + feats - 2)

    @pl.loop(1, regions)
    def _(step):
        pltpu.make_async_remote_copy(
            enc_stage.at[step], enc_in.at[me], send_sem.at[0], recv_sem.at[0],
            device_id=(region_peer(step), my_feat), device_id_type=MESH,
        ).start()

    @pl.loop(1, regions)
    def _(step):
        pltpu.make_async_remote_copy(
            want_out.at[region_peer(step)], want_in.at[me], send_sem.at[1], recv_sem.at[1],
            device_id=(region_peer(step), my_feat), device_id_type=MESH,
        ).start()

    @pl.loop(1, feats)
    def _(step):
        peer = (me, feat_peer(step))
        pltpu.make_async_remote_copy(
            w_stage, w_all.at[:, mine, :], send_sem.at[2], recv_sem.at[2],
            device_id=peer, device_id_type=MESH,
        ).start()
        pltpu.make_async_remote_copy(
            v_stage, v_all.at[mine, :], send_sem.at[3], recv_sem.at[3],
            device_id=peer, device_id_type=MESH,
        ).start()

    sent.append((enc_stage.at[pl.ds(1, regions - 1)], 0))
    sent.append((want_in.at[pl.ds(0, regions - 1)], 1))
    sent.append((w_all.at[:, pl.ds(0, width - rows), :], 2))
    sent.append((v_all.at[pl.ds(0, width - rows), :], 3))

    for load in loads[10:]:
        load.wait()

    def build_tiles(block):
        pores = lax.broadcasted_iota(jnp.int32, (BLOCK, BLOCK), 0)
        for column in range(NBR):
            src = edge_src[block, column : column + 1, :]
            dst = edge_dst[block, column : column + 1, :]
            weight = cond[block, column : column + 1, :].astype(jnp.float32)
            src_hot = jnp.where(pores == src, 1.0, 0.0).astype(jnp.bfloat16)
            dst_hot = jnp.where(pores == dst, weight, 0.0).astype(jnp.bfloat16)
            tiles[block, column * BLOCK : (column + 1) * BLOCK, :] = lax.dot_general(
                src_hot, dst_hot, NT, preferred_element_type=jnp.float32
            ).astype(jnp.bfloat16)

    early = blocks // 8

    @pl.loop(0, early, unroll=min(4, early))
    def _(block):
        build_tiles(block)

    wait_bytes(enc_in.at[pl.ds(0, regions - 1)], recv_sem.at[0])

    load_slots.wait()

    @pl.loop(0, blocks)
    def _(slot):
        value = enc_in[slot_of[0, slot]]
        state0[slot] = value
        ext0[slot] = value

    wait_bytes(want_in.at[pl.ds(0, regions - 1)], recv_sem.at[1])
    to_smem = pltpu.make_async_copy(want_in, want_smem, local_sem.at[15])
    to_smem.start()
    to_smem.wait()

    def stage_halo(step, source, first, halo):
        region = region_peer(step)
        for panel in range(CAPACITY):
            entry = want_smem[region, 0, panel]
            halo[step, panel] = source[first + entry]

    def send_halo(step, halo, ext, index):
        pltpu.make_async_remote_copy(
            halo.at[step], ext.at[pl.ds(blocks + me * CAPACITY, CAPACITY)],
            send_sem.at[index], recv_sem.at[index],
            device_id=(region_peer(step), my_feat), device_id_type=MESH,
        ).start()

    def exchange_halo(source, first, halo, ext, index):
        @pl.loop(1, regions)
        def _(step):
            stage_halo(step, source, first, halo)
            send_halo(step, halo, ext, index)

        sent.append((halo.at[pl.ds(1, regions - 1)], index))
        stage_halo(0, source, first, halo)
        for panel in range(CAPACITY):
            ext[blocks + me * CAPACITY + panel] = halo[0, panel]

    exchange_halo(state0, exports, halo0, ext0, 4)

    def share(side):
        def from_peer(step):
            return pl.ds(side * exports + feat_peer(step) * half, half)

        return from_peer

    def to_owner(source, x, side, first_row, index):
        into = pl.ds(pl.multiple_of(first_row + my_feat * rows, rows), rows)
        where = share(side)

        @pl.loop(1, feats)
        def _(step):
            pltpu.make_async_remote_copy(
                source.at[where(step)], x.at[side, :, into, :],
                send_sem.at[index], recv_sem.at[index],
                device_id=(me, feat_peer(step)), device_id_type=MESH,
            ).start()

        sent.append((state0.at[pl.ds(0, half * (feats - 1))], index))
        x[side, :, into, :] = source[where(0)]

    to_owner(state0, x0, 1, 0, 5)
    to_owner(state0, x0, 0, 0, 6)

    @pl.loop(early, blocks, unroll=min(4, early))
    def _(block):
        build_tiles(block)

    wait_bytes(w_all.at[:, pl.ds(0, width - rows), :], recv_sem.at[2])
    wait_bytes(v_all.at[pl.ds(0, width - rows), :], recv_sem.at[3])
    eye_all = (
        lax.broadcasted_iota(jnp.int32, (width, width), 0)
        == lax.broadcasted_iota(jnp.int32, (width, width), 1)
    ).astype(jnp.bfloat16)
    for layer in range(LAYERS):
        w_out_all[layer] = lax.dot_general(
            eye_all, w_all[layer, :, 2 * width :], NT, preferred_element_type=jnp.float32
        ).astype(jnp.bfloat16)

    def aggregate(ext, message, side):
        @pl.loop(side * exports, (side + 1) * exports, unroll=min(8, exports))
        def _(block):
            sources = jnp.concatenate(
                [ext[neighbours[column, block]] for column in range(NBR)], axis=1
            )
            message[block] = jnp.dot(
                sources, tiles[block], preferred_element_type=jnp.float32
            ).astype(jnp.bfloat16)

    def update(x, side, layer):
        both = jnp.concatenate([x[side, j] for j in range(half)], axis=1)
        vectors = v_all[...]
        pre = jnp.dot(w_all[layer, :, 0 : 2 * width], both, preferred_element_type=jnp.float32)
        inner = jnp.maximum(pre + vectors[:, layer : layer + 1], 0.0).astype(jnp.bfloat16)
        y = jnp.dot(w_out_all[layer], inner, preferred_element_type=jnp.float32)
        mean = jnp.mean(y, axis=0, keepdims=True)
        shifted = y - mean
        var = jnp.mean(shifted * shifted, axis=0, keepdims=True)
        normed = shifted * lax.rsqrt(var + 1e-05)
        change = normed * vectors[:, 2 + layer : 3 + layer] + vectors[:, 4 + layer : 5 + layer]
        return (both[0:width].astype(jnp.float32) + change).astype(jnp.bfloat16)

    def wait_owner(x, side, index):
        wait_bytes(x.at[side, :, pl.ds(0, width - rows), :], recv_sem.at[index])

    def give_back(x, into, side, first, index):
        where = pl.ds(first + my_feat * half, half)

        def part(step):
            return x.at[side, :, pl.ds(pl.multiple_of(feat_peer(step) * rows, rows), rows), :]

        @pl.loop(1, feats)
        def _(step):
            pltpu.make_async_remote_copy(
                part(step), into.at[where], send_sem.at[index], recv_sem.at[index],
                device_id=(me, feat_peer(step)), device_id_type=MESH,
            ).start()

        sent.append((state0.at[pl.ds(0, half * (feats - 1))], index))
        into[where] = part(0)[...]

    def wait_back(into, index):
        wait_bytes(into.at[pl.ds(0, half * (feats - 1))], recv_sem.at[index])

    halo_bytes = pl.ds(0, (regions - 1) * CAPACITY)
    wait_bytes(ext0.at[halo_bytes], recv_sem.at[4])
    for side in (1, 0):
        aggregate(ext0, message0, side)
        to_owner(message0, x0, side, width, 8 - side)
    for side, into in ((1, exports1), (0, others1)):
        wait_owner(x0, side, 6 - side)
        wait_owner(x0, side, 8 - side)
        new = update(x0, side, 0)
        for j in range(half):
            x1[side, j, 0:width, :] = new[:, j * BLOCK : (j + 1) * BLOCK]
        give_back(x1, into, side, 0, 10 - side)

    wait_back(exports1, 9)
    exchange_halo(exports1, 0, halo1, ext1, 11)
    ext1[pl.ds(exports, exports)] = exports1[...]
    wait_back(others1, 10)
    ext1[pl.ds(0, exports)] = others1[...]
    wait_bytes(ext1.at[halo_bytes], recv_sem.at[11])
    for side in (1, 0):
        aggregate(ext1, message1, side)
        to_owner(message1, x1, side, width, 13 - side)
    for side in (1, 0):
        wait_owner(x1, side, 13 - side)
        new = update(x1, side, 1)
        scaled = v_all[:, 6:7] * new.astype(jnp.float32)
        total = jnp.sum(scaled, axis=0, keepdims=True)
        for j in range(half):
            renewed[side, j] = new[:, j * BLOCK : (j + 1) * BLOCK]
            press_stage[0, side * half + j : side * half + j + 1, :] = (
                total[:, j * BLOCK : (j + 1) * BLOCK]
            )
        give_back(renewed, final, side, side * exports, 15 - side)

    @pl.loop(1, feats)
    def _(step):
        pltpu.make_async_remote_copy(
            press_stage, press_in.at[pl.ds(my_feat, 1)], send_sem.at[16], recv_sem.at[16],
            device_id=(me, feat_peer(step)), device_id_type=MESH,
        ).start()

    sent.append((press_in.at[pl.ds(0, feats - 1)], 16))
    press_in[pl.ds(my_feat, 1)] = press_stage[...]
    wait_back(final, 14)
    wait_back(final, 15)
    for block in range(blocks):
        hidden[:, block * BLOCK : (block + 1) * BLOCK] = final[block]
    wait_bytes(press_in.at[pl.ds(0, feats - 1)], recv_sem.at[16])
    for feat in range(feats):
        for side in range(2):
            first = side * exports + feat * half
            pressure[first : first + half, :] = press_in[feat, side * half : (side + 1) * half, :]

    drain()


def on_device(
    enc_feat, send_order, recv_slot, want, neighbours, edge_src, edge_dst, conductance,
    w_in_h, w_in_m, bias_in, w_out, ln_gain, ln_shift, w_read,
):
    regions = lax.axis_size("region")
    feats = lax.axis_size("feat")
    rows, nodes = enc_feat.shape
    blocks = neighbours.shape[0]
    exports = blocks // 2
    width = rows * feats
    own = blocks // feats
    half = own // 2
    panels = regions * CAPACITY
    bf16, f32, i32 = jnp.bfloat16, jnp.float32, jnp.int32
    vmem = pl.BlockSpec(memory_space=pltpu.VMEM)
    phases = 17
    hidden, pressure = pl.pallas_call(
        network_kernel,
        out_shape=(
            jax.ShapeDtypeStruct((rows, nodes), bf16),
            jax.ShapeDtypeStruct((blocks, BLOCK), f32),
        ),
        in_specs=[pl.BlockSpec(memory_space=pltpu.HBM)] * 15,
        out_specs=(vmem, vmem),
        scratch_shapes=[
            pltpu.SMEM((1, blocks), i32),
            pltpu.SMEM((1, regions), i32),
            pltpu.SMEM((NBR, blocks), i32),
            pltpu.SMEM((CAPACITY, regions), i32),
            pltpu.VMEM((regions, 1, BLOCK), i32),
            pltpu.VMEM((1, BLOCK), i32),
            pltpu.SMEM((1, BLOCK), i32),
            pltpu.VMEM((LAYERS, rows, width), bf16),
            pltpu.VMEM((LAYERS, rows, width), bf16),
            pltpu.VMEM((LAYERS, rows, width), bf16),
            pltpu.VMEM((LAYERS, rows), f32),
            pltpu.VMEM((LAYERS, rows), f32),
            pltpu.VMEM((LAYERS, rows), f32),
            pltpu.VMEM((1, rows), f32),
            pltpu.VMEM((blocks, rows, BLOCK), bf16),
            pltpu.VMEM((blocks, NBR, BLOCK), i32),
            pltpu.VMEM((blocks, NBR, BLOCK), i32),
            pltpu.VMEM((blocks, NBR, BLOCK), bf16),
            pltpu.VMEM((regions, rows, BLOCK), bf16),
            pltpu.VMEM((regions, rows, BLOCK), bf16),
            pltpu.VMEM((regions, 1, BLOCK), i32),
            pltpu.SMEM((regions, 1, BLOCK), i32),
            pltpu.VMEM((blocks, rows, BLOCK), bf16),
            pltpu.VMEM((blocks + panels, rows, BLOCK), bf16),
            pltpu.VMEM((blocks + panels, rows, BLOCK), bf16),
            pltpu.VMEM((regions, CAPACITY, rows, BLOCK), bf16),
            pltpu.VMEM((regions, CAPACITY, rows, BLOCK), bf16),
            pltpu.VMEM((blocks, NBR * BLOCK, BLOCK), bf16),
            pltpu.VMEM((blocks, rows, BLOCK), bf16),
            pltpu.VMEM((blocks, rows, BLOCK), bf16),
            pltpu.VMEM((2, half, 2 * width, BLOCK), bf16),
            pltpu.VMEM((2, half, 2 * width, BLOCK), bf16),
            pltpu.VMEM((2, half, width, BLOCK), bf16),
            pltpu.VMEM((exports, rows, BLOCK), bf16),
            pltpu.VMEM((exports, rows, BLOCK), bf16),
            pltpu.VMEM((blocks, rows, BLOCK), bf16),
            pltpu.VMEM((1, own, BLOCK), f32),
            pltpu.VMEM((feats, own, BLOCK), f32),
            pltpu.VMEM((LAYERS, rows, 3 * width), bf16),
            pltpu.VMEM((LAYERS, width, 3 * width), bf16),
            pltpu.VMEM((8, rows), f32),
            pltpu.VMEM((rows, BLOCK), f32),
            pltpu.VMEM((width, BLOCK), f32),
            pltpu.VMEM((LAYERS, width, width), bf16),
            pltpu.SemaphoreType.DMA((17,)),
            pltpu.SemaphoreType.DMA((phases,)),
            pltpu.SemaphoreType.DMA((phases,)),
        ],
        compiler_params=pltpu.CompilerParams(
            collective_id=0, has_side_effects=True, vmem_limit_bytes=60 * 1024 * 1024
        ),
        cost_estimate=pl.CostEstimate(
            flops=2 * blocks * NBR * BLOCK * BLOCK * (BLOCK + 2 * rows),
            bytes_accessed=2**20, transcendentals=0,
        ),
    )(
        send_order, recv_slot, neighbours.T, want.reshape(regions, CAPACITY).T, enc_feat,
        edge_src, edge_dst, conductance, w_in_h, w_in_m, jnp.swapaxes(w_out, 1, 2), bias_in, ln_gain, ln_shift, w_read.reshape(1, rows),
    )
    return hidden, pressure.reshape(nodes)


def solution(mesh):
    return jax.shard_map(
        on_device,
        mesh=mesh,
        in_specs=(
            P("feat", "region"),
            P("region", None),
            P("region", None),
            P("region", None, None),
            P("region", None),
            P("region", None, None),
            P("region", None, None),
            P("region", None, None),
            P(None, "feat", None),
            P(None, "feat", None),
            P(None, "feat"),
            P(None, None, "feat"),
            P(None, "feat"),
            P(None, "feat"),
            P("feat"),
        ),
        out_specs=(P("feat", "region"), P("region")),
        check_vma=False,
    )
```

```python
import functools

import jax
import jax.numpy as jnp
from jax import lax
from jax.experimental import pallas as pl
from jax.experimental.pallas import tpu as pltpu
from jax.sharding import PartitionSpec as P

BLOCK = 128
NBR = 8
CAPACITY = 4
LAYERS = 2
MESH = pl.DeviceIdType.MESH
NT = (((1,), (1,)), ((), ()))


def wait_bytes(ref, sem):
    pltpu.make_async_copy(ref, ref, sem).wait()


def network_kernel(
    order_hbm, slot_hbm, nbr_hbm, want_hbm, enc_hbm, src_hbm, dst_hbm, cond_hbm,
    w_in_h_hbm, w_in_m_hbm, w_out_hbm, bias_hbm, gain_hbm, shift_hbm, read_hbm,
    hidden, pressure,
    send_order, recv_slot, neighbours, want_row, want_out, inverse, slot_of,
    w_in_h, w_in_m, w_out, bias_in, ln_gain, ln_shift, w_read,
    enc, edge_src, edge_dst, cond, enc_stage, enc_in, want_in, want_smem,
    state0, ext0, ext1, halo0, halo1, tiles, message0, message1, x0, x1, renewed,
    exports1, others1, final, press_stage, press_in,
    w_stage, w_all, v_rows, v_stage, v_all, v_wide, w_out_all,
    local_sem, send_sem, recv_sem,
):
    regions = lax.axis_size("region")
    feats = lax.axis_size("feat")
    me = lax.axis_index("region")
    my_feat = lax.axis_index("feat")
    blocks = enc.shape[0]
    exports = blocks // 2
    rows = enc.shape[1]
    width = rows * feats
    half = blocks // feats // 2

    sent = []

    def drain():
        for ref, index in sent:
            wait_bytes(ref, send_sem.at[index])

    loads_enc = [
        pltpu.make_async_copy(
            enc_hbm.at[:, block * BLOCK : (block + 1) * BLOCK], enc.at[block], local_sem.at[0]
        )
        for block in range(blocks)
    ]
    small = (
        (order_hbm, send_order), (slot_hbm, recv_slot), (want_hbm, want_row),
        (w_in_h_hbm, w_in_h), (w_in_m_hbm, w_in_m), (w_out_hbm, w_out), (bias_hbm, bias_in),
        (gain_hbm, ln_gain), (shift_hbm, ln_shift), (read_hbm, w_read),
        (src_hbm, edge_src), (dst_hbm, edge_dst), (cond_hbm, cond), (nbr_hbm, neighbours),
    )
    loads = [
        pltpu.make_async_copy(source, target, local_sem.at[1 + at])
        for at, (source, target) in enumerate(small)
    ]
    for load in (loads[0], *loads_enc):
        load.start()

    depth = 8 if regions % 8 == 0 else regions
    lines = regions // depth

    def apart(order, count):
        return lax.rem(count + count // 2 + (order + 1) // 2 * (1 - 2 * lax.rem(order, 2)), count)

    def region_peer(step):
        line = lax.rem(me // depth + apart(step // depth, lines), lines)
        return line * depth + lax.rem(me + apart(lax.rem(step, depth), depth), depth)

    itself = regions - 1

    def feat_peer(step):
        return lax.rem(my_feat + step, feats)

    barrier = pltpu.get_barrier_semaphore()

    @pl.loop(0, itself)
    def _(step):
        pl.semaphore_signal(barrier, inc=1, device_id=(region_peer(step), my_feat), device_id_type=MESH)

    @pl.loop(1, feats, unroll=feats - 1)
    def _(step):
        pl.semaphore_signal(barrier, inc=1, device_id=(me, feat_peer(step)), device_id_type=MESH)

    for load in loads[1:]:
        load.start()
    loads[0].wait()
    wait_bytes(enc, local_sem.at[0])

    @pl.loop(0, regions, unroll=regions)
    def _(step):
        enc_stage[step] = enc[send_order[0, region_peer(step)]]

    enc_in[me] = enc_stage[itself]

    pl.semaphore_wait(barrier, regions + feats - 2)

    @pl.loop(0, itself, unroll=itself)
    def _(step):
        pltpu.make_async_remote_copy(
            enc_stage.at[step], enc_in.at[me], send_sem.at[0], recv_sem.at[0],
            device_id=(region_peer(step), my_feat), device_id_type=MESH,
        ).start()

    loads[2].wait()
    lanes = lax.broadcasted_iota(jnp.int32, (1, BLOCK), 1)

    @pl.loop(0, regions)
    def _(region):
        row = jnp.zeros((1, BLOCK), jnp.int32)
        for panel in range(CAPACITY):
            row = jnp.where(lanes == panel, want_row[panel, region], row)
        want_out[region] = row

    want_in[me] = want_out[me]

    @pl.loop(0, itself, unroll=itself)
    def _(step):
        pltpu.make_async_remote_copy(
            want_out.at[region_peer(step)], want_in.at[me], send_sem.at[1], recv_sem.at[1],
            device_id=(region_peer(step), my_feat), device_id_type=MESH,
        ).start()

    for load in loads[3:10]:
        load.wait()
    eye = (
        lax.broadcasted_iota(jnp.int32, (rows, rows), 0)
        == lax.broadcasted_iota(jnp.int32, (rows, rows), 1)
    )
    mine = pl.ds(pl.multiple_of(my_feat * rows, rows), rows)
    for layer in range(LAYERS):
        w_stage[layer, :, 0:width] = w_in_h[layer]
        w_stage[layer, :, width : 2 * width] = w_in_m[layer]
        w_stage[layer, :, 2 * width :] = w_out[layer]
        w_all[layer, mine, :] = w_stage[layer]
    v_rows[...] = jnp.zeros_like(v_rows)
    v_rows[0:2, :] = bias_in[...]
    v_rows[2:4, :] = ln_gain[...]
    v_rows[4:6, :] = ln_shift[...]
    v_rows[6:7, :] = w_read[...]
    v_stage[...] = jnp.zeros_like(v_stage)
    v_stage[:, 0:8] = lax.dot_general(
        eye.astype(jnp.float32), v_rows[...], NT,
        precision=lax.Precision.HIGHEST, preferred_element_type=jnp.float32,
    )
    v_all[mine, :] = v_stage[...]
    @pl.loop(1, feats, unroll=feats - 1)
    def _(step):
        peer = (me, feat_peer(step))
        pltpu.make_async_remote_copy(
            w_stage, w_all.at[:, mine, :], send_sem.at[2], recv_sem.at[2],
            device_id=peer, device_id_type=MESH,
        ).start()
        pltpu.make_async_remote_copy(
            v_stage, v_all.at[mine, :], send_sem.at[3], recv_sem.at[3],
            device_id=peer, device_id_type=MESH,
        ).start()

    loads[1].wait()
    slots = lax.broadcasted_iota(jnp.int32, inverse.shape, 1)
    found = jnp.zeros(inverse.shape, jnp.int32)
    for source in range(regions):
        found = jnp.where(slots == recv_slot[0, source], source, found)
    inverse[...] = found
    load_slots = pltpu.make_async_copy(inverse, slot_of, local_sem.at[16])
    load_slots.start()

    sent.append((enc_stage.at[pl.ds(0, itself)], 0))
    sent.append((want_in.at[pl.ds(0, regions - 1)], 1))
    sent.append((w_all.at[:, pl.ds(0, width - rows), :], 2))
    sent.append((v_all.at[pl.ds(0, width - rows), :], 3))

    for load in loads[10:]:
        load.wait()

    def build_tiles(block):
        pores = lax.broadcasted_iota(jnp.int32, (BLOCK, BLOCK), 0)
        for column in range(NBR):
            src = edge_src[block, column : column + 1, :]
            dst = edge_dst[block, column : column + 1, :]
            weight = cond[block, column : column + 1, :].astype(jnp.float32)
            src_hot = jnp.where(pores == src, 1.0, 0.0).astype(jnp.bfloat16)
            dst_hot = jnp.where(pores == dst, weight, 0.0).astype(jnp.bfloat16)
            tiles[block, column * BLOCK : (column + 1) * BLOCK, :] = lax.dot_general(
                src_hot, dst_hot, NT, preferred_element_type=jnp.float32
            ).astype(jnp.bfloat16)

    early = blocks // 8

    @pl.loop(0, early, unroll=min(4, early))
    def _(block):
        build_tiles(block)

    wait_bytes(enc_in.at[pl.ds(0, regions - 1)], recv_sem.at[0])

    load_slots.wait()

    @pl.loop(0, blocks, unroll=min(8, blocks))
    def _(slot):
        value = enc_in[slot_of[0, slot]]
        state0[slot] = value
        ext0[slot] = value

    wait_bytes(want_in.at[pl.ds(0, regions - 1)], recv_sem.at[1])
    to_smem = pltpu.make_async_copy(want_in, want_smem, local_sem.at[15])
    to_smem.start()
    to_smem.wait()

    def stage_halo(step, source, first, halo):
        region = region_peer(step)
        for panel in range(CAPACITY):
            entry = want_smem[region, 0, panel]
            halo[step, panel] = source[first + entry]

    def send_halo(step, halo, ext, index):
        pltpu.make_async_remote_copy(
            halo.at[step], ext.at[pl.ds(blocks + me * CAPACITY, CAPACITY)],
            send_sem.at[index], recv_sem.at[index],
            device_id=(region_peer(step), my_feat), device_id_type=MESH,
        ).start()

    def exchange_halo(source, first, halo, ext, index):
        @pl.loop(0, itself, unroll=itself)
        def _(step):
            stage_halo(step, source, first, halo)
            send_halo(step, halo, ext, index)

        sent.append((halo.at[pl.ds(0, itself)], index))
        stage_halo(itself, source, first, halo)
        for panel in range(CAPACITY):
            ext[blocks + me * CAPACITY + panel] = halo[itself, panel]

    exchange_halo(state0, exports, halo0, ext0, 4)

    def share(side):
        def from_peer(step):
            return pl.ds(side * exports + feat_peer(step) * half, half)

        return from_peer

    def to_owner(source, x, side, first_row, index):
        into = pl.ds(pl.multiple_of(first_row + my_feat * rows, rows), rows)
        where = share(side)

        @pl.loop(1, feats, unroll=feats - 1)
        def _(step):
            pltpu.make_async_remote_copy(
                source.at[where(step)], x.at[side, :, into, :],
                send_sem.at[index], recv_sem.at[index],
                device_id=(me, feat_peer(step)), device_id_type=MESH,
            ).start()

        sent.append((state0.at[pl.ds(0, half * (feats - 1))], index))
        x[side, :, into, :] = source[where(0)]

    to_owner(state0, x0, 1, 0, 5)
    to_owner(state0, x0, 0, 0, 6)

    @pl.loop(early, blocks, unroll=min(4, early))
    def _(block):
        build_tiles(block)

    wait_bytes(w_all.at[:, pl.ds(0, width - rows), :], recv_sem.at[2])
    wait_bytes(v_all.at[pl.ds(0, width - rows), :], recv_sem.at[3])
    eye_all = (
        lax.broadcasted_iota(jnp.int32, (width, width), 0)
        == lax.broadcasted_iota(jnp.int32, (width, width), 1)
    ).astype(jnp.bfloat16)
    for layer in range(LAYERS):
        w_out_all[layer] = lax.dot_general(
            eye_all, w_all[layer, :, 2 * width :], NT, preferred_element_type=jnp.float32
        ).astype(jnp.bfloat16)

    for vector in range(7):
        v_wide[vector] = jnp.broadcast_to(v_all[:, vector : vector + 1], (width, BLOCK))

    def wide(vector):
        return jnp.concatenate([v_wide[vector]] * half, axis=1)

    def aggregate(ext, message, side):
        @pl.loop(side * exports, (side + 1) * exports, unroll=min(16, exports))
        def _(block):
            sources = jnp.concatenate(
                [ext[neighbours[column, block]] for column in range(NBR)], axis=1
            )
            message[block] = jnp.dot(
                sources, tiles[block], preferred_element_type=jnp.float32
            ).astype(jnp.bfloat16)

    def update(x, side, layer):
        both = jnp.concatenate([x[side, j] for j in range(half)], axis=1)
        pre = jnp.dot(w_all[layer, :, 0 : 2 * width], both, preferred_element_type=jnp.float32)
        inner = jnp.maximum(pre + wide(layer), 0.0).astype(jnp.bfloat16)
        y = jnp.dot(w_out_all[layer], inner, preferred_element_type=jnp.float32)
        mean = jnp.mean(y, axis=0, keepdims=True)
        shifted = y - mean
        var = jnp.mean(shifted * shifted, axis=0, keepdims=True)
        normed = shifted * lax.rsqrt(var + 1e-05)
        change = normed * wide(2 + layer) + wide(4 + layer)
        return (both[0:width].astype(jnp.float32) + change).astype(jnp.bfloat16)

    def wait_owner(x, side, index):
        wait_bytes(x.at[side, :, pl.ds(0, width - rows), :], recv_sem.at[index])

    def give_back(x, into, side, first, index):
        where = pl.ds(first + my_feat * half, half)

        def part(step):
            return x.at[side, :, pl.ds(pl.multiple_of(feat_peer(step) * rows, rows), rows), :]

        @pl.loop(1, feats, unroll=feats - 1)
        def _(step):
            pltpu.make_async_remote_copy(
                part(step), into.at[where], send_sem.at[index], recv_sem.at[index],
                device_id=(me, feat_peer(step)), device_id_type=MESH,
            ).start()

        sent.append((state0.at[pl.ds(0, half * (feats - 1))], index))
        into[where] = part(0)[...]

    def wait_back(into, index):
        wait_bytes(into.at[pl.ds(0, half * (feats - 1))], recv_sem.at[index])

    halo_bytes = pl.ds(0, (regions - 1) * CAPACITY)
    wait_bytes(ext0.at[halo_bytes], recv_sem.at[4])
    for side in (1, 0):
        aggregate(ext0, message0, side)
        to_owner(message0, x0, side, width, 8 - side)
    for side, into in ((1, exports1), (0, others1)):
        wait_owner(x0, side, 6 - side)
        wait_owner(x0, side, 8 - side)
        new = update(x0, side, 0)
        for j in range(half):
            x1[side, j, 0:width, :] = new[:, j * BLOCK : (j + 1) * BLOCK]
        give_back(x1, into, side, 0, 10 - side)

    wait_back(exports1, 9)
    exchange_halo(exports1, 0, halo1, ext1, 11)
    ext1[pl.ds(exports, exports)] = exports1[...]
    wait_back(others1, 10)
    ext1[pl.ds(0, exports)] = others1[...]
    wait_bytes(ext1.at[halo_bytes], recv_sem.at[11])
    for side in (1, 0):
        aggregate(ext1, message1, side)
        to_owner(message1, x1, side, width, 13 - side)
    for side in (1, 0):
        wait_owner(x1, side, 13 - side)
        new = update(x1, side, 1)
        scaled = wide(6) * new.astype(jnp.float32)
        total = jnp.sum(scaled, axis=0, keepdims=True)
        for j in range(half):
            renewed[side, j] = new[:, j * BLOCK : (j + 1) * BLOCK]
            press_stage[0, side * half + j : side * half + j + 1, :] = (
                total[:, j * BLOCK : (j + 1) * BLOCK]
            )
        give_back(renewed, final, side, side * exports, 15 - side)

    @pl.loop(1, feats, unroll=feats - 1)
    def _(step):
        pltpu.make_async_remote_copy(
            press_stage, press_in.at[pl.ds(my_feat, 1)], send_sem.at[16], recv_sem.at[16],
            device_id=(me, feat_peer(step)), device_id_type=MESH,
        ).start()

    sent.append((press_in.at[pl.ds(0, feats - 1)], 16))
    press_in[pl.ds(my_feat, 1)] = press_stage[...]
    wait_back(final, 14)
    wait_back(final, 15)
    for block in range(blocks):
        hidden[:, block * BLOCK : (block + 1) * BLOCK] = final[block]
    wait_bytes(press_in.at[pl.ds(0, feats - 1)], recv_sem.at[16])
    for feat in range(feats):
        for side in range(2):
            first = side * exports + feat * half
            pressure[first : first + half, :] = press_in[feat, side * half : (side + 1) * half, :]

    drain()


def on_device(
    enc_feat, send_order, recv_slot, want, neighbours, edge_src, edge_dst, conductance,
    w_in_h, w_in_m, bias_in, w_out, ln_gain, ln_shift, w_read,
):
    regions = lax.axis_size("region")
    feats = lax.axis_size("feat")
    rows, nodes = enc_feat.shape
    blocks = neighbours.shape[0]
    exports = blocks // 2
    width = rows * feats
    own = blocks // feats
    half = own // 2
    panels = regions * CAPACITY
    bf16, f32, i32 = jnp.bfloat16, jnp.float32, jnp.int32
    vmem = pl.BlockSpec(memory_space=pltpu.VMEM)
    phases = 17
    hidden, pressure = pl.pallas_call(
        network_kernel,
        out_shape=(
            jax.ShapeDtypeStruct((rows, nodes), bf16),
            jax.ShapeDtypeStruct((blocks, BLOCK), f32),
        ),
        in_specs=[pl.BlockSpec(memory_space=pltpu.HBM)] * 15,
        out_specs=(vmem, vmem),
        scratch_shapes=[
            pltpu.SMEM((1, blocks), i32),
            pltpu.SMEM((1, regions), i32),
            pltpu.SMEM((NBR, blocks), i32),
            pltpu.SMEM((CAPACITY, regions), i32),
            pltpu.VMEM((regions, 1, BLOCK), i32),
            pltpu.VMEM((1, BLOCK), i32),
            pltpu.SMEM((1, BLOCK), i32),
            pltpu.VMEM((LAYERS, rows, width), bf16),
            pltpu.VMEM((LAYERS, rows, width), bf16),
            pltpu.VMEM((LAYERS, rows, width), bf16),
            pltpu.VMEM((LAYERS, rows), f32),
            pltpu.VMEM((LAYERS, rows), f32),
            pltpu.VMEM((LAYERS, rows), f32),
            pltpu.VMEM((1, rows), f32),
            pltpu.VMEM((blocks, rows, BLOCK), bf16),
            pltpu.VMEM((blocks, NBR, BLOCK), i32),
            pltpu.VMEM((blocks, NBR, BLOCK), i32),
            pltpu.VMEM((blocks, NBR, BLOCK), bf16),
            pltpu.VMEM((regions, rows, BLOCK), bf16),
            pltpu.VMEM((regions, rows, BLOCK), bf16),
            pltpu.VMEM((regions, 1, BLOCK), i32),
            pltpu.SMEM((regions, 1, BLOCK), i32),
            pltpu.VMEM((blocks, rows, BLOCK), bf16),
            pltpu.VMEM((blocks + panels, rows, BLOCK), bf16),
            pltpu.VMEM((blocks + panels, rows, BLOCK), bf16),
            pltpu.VMEM((regions, CAPACITY, rows, BLOCK), bf16),
            pltpu.VMEM((regions, CAPACITY, rows, BLOCK), bf16),
            pltpu.VMEM((blocks, NBR * BLOCK, BLOCK), bf16),
            pltpu.VMEM((blocks, rows, BLOCK), bf16),
            pltpu.VMEM((blocks, rows, BLOCK), bf16),
            pltpu.VMEM((2, half, 2 * width, BLOCK), bf16),
            pltpu.VMEM((2, half, 2 * width, BLOCK), bf16),
            pltpu.VMEM((2, half, width, BLOCK), bf16),
            pltpu.VMEM((exports, rows, BLOCK), bf16),
            pltpu.VMEM((exports, rows, BLOCK), bf16),
            pltpu.VMEM((blocks, rows, BLOCK), bf16),
            pltpu.VMEM((1, own, BLOCK), f32),
            pltpu.VMEM((feats, own, BLOCK), f32),
            pltpu.VMEM((LAYERS, rows, 3 * width), bf16),
            pltpu.VMEM((LAYERS, width, 3 * width), bf16),
            pltpu.VMEM((8, rows), f32),
            pltpu.VMEM((rows, BLOCK), f32),
            pltpu.VMEM((width, BLOCK), f32),
            pltpu.VMEM((7, width, BLOCK), f32),
            pltpu.VMEM((LAYERS, width, width), bf16),
            pltpu.SemaphoreType.DMA((17,)),
            pltpu.SemaphoreType.DMA((phases,)),
            pltpu.SemaphoreType.DMA((phases,)),
        ],
        compiler_params=pltpu.CompilerParams(
            collective_id=0, has_side_effects=True, vmem_limit_bytes=60 * 1024 * 1024
        ),
        cost_estimate=pl.CostEstimate(
            flops=2 * blocks * NBR * BLOCK * BLOCK * (BLOCK + 2 * rows),
            bytes_accessed=2**20, transcendentals=0,
        ),
    )(
        send_order, recv_slot, neighbours.T, want.reshape(regions, CAPACITY).T, enc_feat,
        edge_src, edge_dst, conductance, w_in_h, w_in_m, jnp.swapaxes(w_out, 1, 2), bias_in, ln_gain, ln_shift, w_read.reshape(1, rows),
    )
    return hidden, pressure.reshape(nodes)


def solution(mesh):
    return jax.shard_map(
        on_device,
        mesh=mesh,
        in_specs=(
            P("feat", "region"),
            P("region", None),
            P("region", None),
            P("region", None, None),
            P("region", None),
            P("region", None, None),
            P("region", None, None),
            P("region", None, None),
            P(None, "feat", None),
            P(None, "feat", None),
            P(None, "feat"),
            P(None, None, "feat"),
            P(None, "feat"),
            P(None, "feat"),
            P("feat"),
        ),
        out_specs=(P("feat", "region"), P("region")),
        check_vma=False,
    )
```

```python
import functools

import jax
import jax.numpy as jnp
from jax import lax
from jax.experimental import pallas as pl
from jax.experimental.pallas import tpu as pltpu
from jax.sharding import PartitionSpec as P

BLOCK = 128
NBR = 8
CAPACITY = 4
LAYERS = 2
MESH = pl.DeviceIdType.MESH
NT = (((1,), (1,)), ((), ()))


def wait_bytes(ref, sem):
    pltpu.make_async_copy(ref, ref, sem).wait()


def network_kernel(
    order_hbm, slot_hbm, nbr_hbm, want_hbm, enc_hbm, src_hbm, dst_hbm, cond_hbm,
    w_in_h_hbm, w_in_m_hbm, w_out_hbm, bias_hbm, gain_hbm, shift_hbm, read_hbm,
    hidden, pressure,
    send_order, recv_slot, neighbours, want_row, want_out, inverse, slot_of,
    w_in_h, w_in_m, w_out, bias_in, ln_gain, ln_shift, w_read,
    enc, edge_src, edge_dst, cond, enc_stage, enc_in, want_in, want_all, want_smem,
    state0, ext0, ext1, halo0, halo1, tiles, message0, message1, x0, x1, renewed,
    exports1, others1, final, press_stage, press_in,
    w_stage, w_all, v_rows, v_stage, v_all, v_wide, w_out_all,
    local_sem, send_sem, recv_sem,
):
    regions = lax.axis_size("region")
    feats = lax.axis_size("feat")
    me = lax.axis_index("region")
    my_feat = lax.axis_index("feat")
    blocks = enc.shape[0]
    exports = blocks // 2
    rows = enc.shape[1]
    width = rows * feats
    half = blocks // feats // 2

    sent = []

    def drain():
        for ref, index in sent:
            wait_bytes(ref, send_sem.at[index])

    loads_enc = [
        pltpu.make_async_copy(
            enc_hbm.at[:, block * BLOCK : (block + 1) * BLOCK], enc.at[block], local_sem.at[0]
        )
        for block in range(blocks)
    ]
    small = (
        (order_hbm, send_order), (slot_hbm, recv_slot), (want_hbm, want_row),
        (w_in_h_hbm, w_in_h), (w_in_m_hbm, w_in_m), (w_out_hbm, w_out), (bias_hbm, bias_in),
        (gain_hbm, ln_gain), (shift_hbm, ln_shift), (read_hbm, w_read),
        (src_hbm, edge_src), (dst_hbm, edge_dst), (cond_hbm, cond), (nbr_hbm, neighbours),
    )
    loads = [
        pltpu.make_async_copy(source, target, local_sem.at[1 + at])
        for at, (source, target) in enumerate(small)
    ]
    depth = 8 if regions % 8 == 0 else regions
    lines = regions // depth

    def apart(order, count):
        return lax.rem(count + count // 2 + (order + 1) // 2 * (1 - 2 * lax.rem(order, 2)), count)

    def region_peer(step):
        line = lax.rem(me // depth + apart(step // depth, lines), lines)
        return line * depth + lax.rem(me + apart(lax.rem(step, depth), depth), depth)

    itself = regions - 1

    def feat_peer(step):
        return lax.rem(my_feat + step, feats)

    barrier = pltpu.get_barrier_semaphore()

    @pl.loop(0, itself, unroll=itself)
    def _(step):
        pl.semaphore_signal(barrier, inc=1, device_id=(region_peer(step), my_feat), device_id_type=MESH)

    @pl.loop(1, feats, unroll=feats - 1)
    def _(step):
        pl.semaphore_signal(barrier, inc=1, device_id=(me, feat_peer(step)), device_id_type=MESH)

    for load in (loads[0], loads[2], loads[1], *loads_enc, *loads[3:]):
        load.start()
    loads[0].wait()
    wait_bytes(enc, local_sem.at[0])

    @pl.loop(0, regions, unroll=regions)
    def _(step):
        enc_stage[step] = enc[send_order[0, region_peer(step)]]

    enc_in[me] = enc_stage[itself]

    loads[2].wait()
    lanes = lax.broadcasted_iota(jnp.int32, (1, BLOCK), 1)

    @pl.loop(0, regions)
    def _(region):
        row = jnp.zeros((1, BLOCK), jnp.int32)
        for panel in range(CAPACITY):
            row = jnp.where(lanes == me * CAPACITY + panel, want_row[panel, region], row)
        want_out[region] = row

    want_in[me] = want_out[me]

    loads[1].wait()
    slots = lax.broadcasted_iota(jnp.int32, inverse.shape, 1)
    found = jnp.zeros(inverse.shape, jnp.int32)
    for source in range(regions):
        found = jnp.where(slots == recv_slot[0, source], source, found)
    inverse[...] = found
    load_slots = pltpu.make_async_copy(inverse, slot_of, local_sem.at[16])
    load_slots.start()

    pl.semaphore_wait(barrier, regions + feats - 2)

    @pl.loop(0, itself, unroll=itself)
    def _(step):
        pltpu.make_async_remote_copy(
            enc_stage.at[step], enc_in.at[me], send_sem.at[0], recv_sem.at[0],
            device_id=(region_peer(step), my_feat), device_id_type=MESH,
        ).start()

    @pl.loop(0, itself, unroll=itself)
    def _(step):
        pltpu.make_async_remote_copy(
            want_out.at[region_peer(step)], want_in.at[me], send_sem.at[1], recv_sem.at[1],
            device_id=(region_peer(step), my_feat), device_id_type=MESH,
        ).start()

    for load in loads[3:10]:
        load.wait()
    eye = (
        lax.broadcasted_iota(jnp.int32, (rows, rows), 0)
        == lax.broadcasted_iota(jnp.int32, (rows, rows), 1)
    )
    mine = pl.ds(pl.multiple_of(my_feat * rows, rows), rows)
    for layer in range(LAYERS):
        w_stage[layer, :, 0:width] = w_in_h[layer]
        w_stage[layer, :, width : 2 * width] = w_in_m[layer]
        w_stage[layer, :, 2 * width :] = w_out[layer]
        w_all[layer, mine, :] = w_stage[layer]
    v_rows[...] = jnp.zeros_like(v_rows)
    v_rows[0:2, :] = bias_in[...]
    v_rows[2:4, :] = ln_gain[...]
    v_rows[4:6, :] = ln_shift[...]
    v_rows[6:7, :] = w_read[...]
    v_stage[...] = jnp.zeros_like(v_stage)
    v_stage[:, 0:8] = lax.dot_general(
        eye.astype(jnp.float32), v_rows[...], NT,
        precision=lax.Precision.HIGHEST, preferred_element_type=jnp.float32,
    )
    v_all[mine, :] = v_stage[...]
    @pl.loop(1, feats, unroll=feats - 1)
    def _(step):
        peer = (me, feat_peer(step))
        pltpu.make_async_remote_copy(
            w_stage, w_all.at[:, mine, :], send_sem.at[2], recv_sem.at[2],
            device_id=peer, device_id_type=MESH,
        ).start()
        pltpu.make_async_remote_copy(
            v_stage, v_all.at[mine, :], send_sem.at[3], recv_sem.at[3],
            device_id=peer, device_id_type=MESH,
        ).start()

    sent.append((enc_stage.at[pl.ds(0, itself)], 0))
    sent.append((want_in.at[pl.ds(0, regions - 1)], 1))
    sent.append((w_all.at[:, pl.ds(0, width - rows), :], 2))
    sent.append((v_all.at[pl.ds(0, width - rows), :], 3))

    for load in loads[10:]:
        load.wait()

    def build_tiles(block):
        pores = lax.broadcasted_iota(jnp.int32, (BLOCK, BLOCK), 0)
        for column in range(NBR):
            src = edge_src[block, column : column + 1, :]
            dst = edge_dst[block, column : column + 1, :]
            weight = cond[block, column : column + 1, :].astype(jnp.float32)
            src_hot = jnp.where(pores == src, 1.0, 0.0).astype(jnp.bfloat16)
            dst_hot = jnp.where(pores == dst, weight, 0.0).astype(jnp.bfloat16)
            tiles[block, column * BLOCK : (column + 1) * BLOCK, :] = lax.dot_general(
                src_hot, dst_hot, NT, preferred_element_type=jnp.float32
            ).astype(jnp.bfloat16)

    early = blocks // 8

    @pl.loop(0, early, unroll=min(4, early))
    def _(block):
        build_tiles(block)

    wait_bytes(enc_in.at[pl.ds(0, regions - 1)], recv_sem.at[0])

    load_slots.wait()

    def place(slot):
        value = enc_in[slot_of[0, slot]]
        state0[slot] = value
        ext0[slot] = value

    pl.loop(exports, blocks, unroll=exports)(place)

    wait_bytes(want_in.at[pl.ds(0, regions - 1)], recv_sem.at[1])
    wants = want_in[0]
    for region in range(1, regions):
        wants = wants + want_in[region]
    want_all[...] = wants
    to_smem = pltpu.make_async_copy(want_all, want_smem, local_sem.at[15])
    to_smem.start()
    to_smem.wait()

    def stage_halo(step, source, first, halo):
        region = region_peer(step)
        for panel in range(CAPACITY):
            entry = want_smem[0, region * CAPACITY + panel]
            halo[step, panel] = source[first + entry]

    def send_halo(step, halo, ext, index):
        pltpu.make_async_remote_copy(
            halo.at[step], ext.at[pl.ds(blocks + me * CAPACITY, CAPACITY)],
            send_sem.at[index], recv_sem.at[index],
            device_id=(region_peer(step), my_feat), device_id_type=MESH,
        ).start()

    def exchange_halo(source, first, halo, ext, index):
        @pl.loop(0, itself, unroll=itself)
        def _(step):
            stage_halo(step, source, first, halo)
            send_halo(step, halo, ext, index)

        sent.append((halo.at[pl.ds(0, itself)], index))
        stage_halo(itself, source, first, halo)
        for panel in range(CAPACITY):
            ext[blocks + me * CAPACITY + panel] = halo[itself, panel]

    exchange_halo(state0, exports, halo0, ext0, 4)

    def share(side):
        def from_peer(step):
            return pl.ds(side * exports + feat_peer(step) * half, half)

        return from_peer

    def to_owner(source, x, side, first_row, index):
        into = pl.ds(pl.multiple_of(first_row + my_feat * rows, rows), rows)
        where = share(side)

        @pl.loop(1, feats, unroll=feats - 1)
        def _(step):
            pltpu.make_async_remote_copy(
                source.at[where(step)], x.at[side, :, into, :],
                send_sem.at[index], recv_sem.at[index],
                device_id=(me, feat_peer(step)), device_id_type=MESH,
            ).start()

        sent.append((state0.at[pl.ds(0, half * (feats - 1))], index))
        x[side, :, into, :] = source[where(0)]

    pl.loop(0, exports, unroll=exports)(place)
    to_owner(state0, x0, 1, 0, 5)
    to_owner(state0, x0, 0, 0, 6)

    @pl.loop(early, blocks, unroll=min(4, early))
    def _(block):
        build_tiles(block)

    wait_bytes(w_all.at[:, pl.ds(0, width - rows), :], recv_sem.at[2])
    wait_bytes(v_all.at[pl.ds(0, width - rows), :], recv_sem.at[3])
    eye_all = (
        lax.broadcasted_iota(jnp.int32, (width, width), 0)
        == lax.broadcasted_iota(jnp.int32, (width, width), 1)
    ).astype(jnp.bfloat16)
    for layer in range(LAYERS):
        w_out_all[layer] = lax.dot_general(
            eye_all, w_all[layer, :, 2 * width :], NT, preferred_element_type=jnp.float32
        ).astype(jnp.bfloat16)

    for vector in range(7):
        v_wide[vector] = jnp.broadcast_to(v_all[:, vector : vector + 1], (width, BLOCK))

    def wide(vector):
        return jnp.concatenate([v_wide[vector]] * half, axis=1)

    def aggregate(ext, message, side):
        @pl.loop(side * exports, (side + 1) * exports, unroll=min(16, exports))
        def _(block):
            sources = jnp.concatenate(
                [ext[neighbours[column, block]] for column in range(NBR)], axis=1
            )
            message[block] = jnp.dot(
                sources, tiles[block], preferred_element_type=jnp.float32
            ).astype(jnp.bfloat16)

    def update(x, side, layer):
        both = jnp.concatenate([x[side, j] for j in range(half)], axis=1)
        pre = jnp.dot(w_all[layer, :, 0 : 2 * width], both, preferred_element_type=jnp.float32)
        inner = jnp.maximum(pre + wide(layer), 0.0).astype(jnp.bfloat16)
        y = jnp.dot(w_out_all[layer], inner, preferred_element_type=jnp.float32)
        mean = jnp.mean(y, axis=0, keepdims=True)
        shifted = y - mean
        var = jnp.mean(shifted * shifted, axis=0, keepdims=True)
        normed = shifted * lax.rsqrt(var + 1e-05)
        change = normed * wide(2 + layer) + wide(4 + layer)
        return (both[0:width].astype(jnp.float32) + change).astype(jnp.bfloat16)

    def wait_owner(x, side, index):
        wait_bytes(x.at[side, :, pl.ds(0, width - rows), :], recv_sem.at[index])

    def give_back(x, into, side, first, index):
        where = pl.ds(first + my_feat * half, half)

        def part(step):
            return x.at[side, :, pl.ds(pl.multiple_of(feat_peer(step) * rows, rows), rows), :]

        @pl.loop(1, feats, unroll=feats - 1)
        def _(step):
            pltpu.make_async_remote_copy(
                part(step), into.at[where], send_sem.at[index], recv_sem.at[index],
                device_id=(me, feat_peer(step)), device_id_type=MESH,
            ).start()

        sent.append((state0.at[pl.ds(0, half * (feats - 1))], index))
        into[where] = part(0)[...]

    def wait_back(into, index):
        wait_bytes(into.at[pl.ds(0, half * (feats - 1))], recv_sem.at[index])

    halo_bytes = pl.ds(0, (regions - 1) * CAPACITY)
    wait_bytes(ext0.at[halo_bytes], recv_sem.at[4])
    for side in (1, 0):
        aggregate(ext0, message0, side)
        to_owner(message0, x0, side, width, 8 - side)
    for side, into in ((1, exports1), (0, others1)):
        wait_owner(x0, side, 6 - side)
        wait_owner(x0, side, 8 - side)
        new = update(x0, side, 0)
        for j in range(half):
            x1[side, j, 0:width, :] = new[:, j * BLOCK : (j + 1) * BLOCK]
        give_back(x1, into, side, 0, 10 - side)

    wait_back(exports1, 9)
    exchange_halo(exports1, 0, halo1, ext1, 11)
    ext1[pl.ds(exports, exports)] = exports1[...]
    wait_back(others1, 10)
    ext1[pl.ds(0, exports)] = others1[...]
    wait_bytes(ext1.at[halo_bytes], recv_sem.at[11])
    for side in (1, 0):
        aggregate(ext1, message1, side)
        to_owner(message1, x1, side, width, 13 - side)
    for side in (1, 0):
        wait_owner(x1, side, 13 - side)
        new = update(x1, side, 1)
        scaled = wide(6) * new.astype(jnp.float32)
        total = jnp.sum(scaled, axis=0, keepdims=True)
        for j in range(half):
            renewed[side, j] = new[:, j * BLOCK : (j + 1) * BLOCK]
            press_stage[0, side * half + j : side * half + j + 1, :] = (
                total[:, j * BLOCK : (j + 1) * BLOCK]
            )
        give_back(renewed, final, side, side * exports, 15 - side)

    @pl.loop(1, feats, unroll=feats - 1)
    def _(step):
        pltpu.make_async_remote_copy(
            press_stage, press_in.at[pl.ds(my_feat, 1)], send_sem.at[16], recv_sem.at[16],
            device_id=(me, feat_peer(step)), device_id_type=MESH,
        ).start()

    sent.append((press_in.at[pl.ds(0, feats - 1)], 16))
    press_in[pl.ds(my_feat, 1)] = press_stage[...]
    wait_back(final, 14)
    wait_back(final, 15)
    for block in range(blocks):
        hidden[:, block * BLOCK : (block + 1) * BLOCK] = final[block]
    wait_bytes(press_in.at[pl.ds(0, feats - 1)], recv_sem.at[16])
    for feat in range(feats):
        for side in range(2):
            first = side * exports + feat * half
            pressure[first : first + half, :] = press_in[feat, side * half : (side + 1) * half, :]

    drain()


def on_device(
    enc_feat, send_order, recv_slot, want, neighbours, edge_src, edge_dst, conductance,
    w_in_h, w_in_m, bias_in, w_out, ln_gain, ln_shift, w_read,
):
    regions = lax.axis_size("region")
    feats = lax.axis_size("feat")
    rows, nodes = enc_feat.shape
    blocks = neighbours.shape[0]
    exports = blocks // 2
    width = rows * feats
    own = blocks // feats
    half = own // 2
    panels = regions * CAPACITY
    bf16, f32, i32 = jnp.bfloat16, jnp.float32, jnp.int32
    vmem = pl.BlockSpec(memory_space=pltpu.VMEM)
    phases = 17
    hidden, pressure = pl.pallas_call(
        network_kernel,
        out_shape=(
            jax.ShapeDtypeStruct((rows, nodes), bf16),
            jax.ShapeDtypeStruct((blocks, BLOCK), f32),
        ),
        in_specs=[pl.BlockSpec(memory_space=pltpu.HBM)] * 15,
        out_specs=(vmem, vmem),
        scratch_shapes=[
            pltpu.SMEM((1, blocks), i32),
            pltpu.SMEM((1, regions), i32),
            pltpu.SMEM((NBR, blocks), i32),
            pltpu.SMEM((CAPACITY, regions), i32),
            pltpu.VMEM((regions, 1, BLOCK), i32),
            pltpu.VMEM((1, BLOCK), i32),
            pltpu.SMEM((1, BLOCK), i32),
            pltpu.VMEM((LAYERS, rows, width), bf16),
            pltpu.VMEM((LAYERS, rows, width), bf16),
            pltpu.VMEM((LAYERS, rows, width), bf16),
            pltpu.VMEM((LAYERS, rows), f32),
            pltpu.VMEM((LAYERS, rows), f32),
            pltpu.VMEM((LAYERS, rows), f32),
            pltpu.VMEM((1, rows), f32),
            pltpu.VMEM((blocks, rows, BLOCK), bf16),
            pltpu.VMEM((blocks, NBR, BLOCK), i32),
            pltpu.VMEM((blocks, NBR, BLOCK), i32),
            pltpu.VMEM((blocks, NBR, BLOCK), bf16),
            pltpu.VMEM((regions, rows, BLOCK), bf16),
            pltpu.VMEM((regions, rows, BLOCK), bf16),
            pltpu.VMEM((regions, 1, BLOCK), i32),
            pltpu.VMEM((1, BLOCK), i32),
            pltpu.SMEM((1, BLOCK), i32),
            pltpu.VMEM((blocks, rows, BLOCK), bf16),
            pltpu.VMEM((blocks + panels, rows, BLOCK), bf16),
            pltpu.VMEM((blocks + panels, rows, BLOCK), bf16),
            pltpu.VMEM((regions, CAPACITY, rows, BLOCK), bf16),
            pltpu.VMEM((regions, CAPACITY, rows, BLOCK), bf16),
            pltpu.VMEM((blocks, NBR * BLOCK, BLOCK), bf16),
            pltpu.VMEM((blocks, rows, BLOCK), bf16),
            pltpu.VMEM((blocks, rows, BLOCK), bf16),
            pltpu.VMEM((2, half, 2 * width, BLOCK), bf16),
            pltpu.VMEM((2, half, 2 * width, BLOCK), bf16),
            pltpu.VMEM((2, half, width, BLOCK), bf16),
            pltpu.VMEM((exports, rows, BLOCK), bf16),
            pltpu.VMEM((exports, rows, BLOCK), bf16),
            pltpu.VMEM((blocks, rows, BLOCK), bf16),
            pltpu.VMEM((1, own, BLOCK), f32),
            pltpu.VMEM((feats, own, BLOCK), f32),
            pltpu.VMEM((LAYERS, rows, 3 * width), bf16),
            pltpu.VMEM((LAYERS, width, 3 * width), bf16),
            pltpu.VMEM((8, rows), f32),
            pltpu.VMEM((rows, BLOCK), f32),
            pltpu.VMEM((width, BLOCK), f32),
            pltpu.VMEM((7, width, BLOCK), f32),
            pltpu.VMEM((LAYERS, width, width), bf16),
            pltpu.SemaphoreType.DMA((17,)),
            pltpu.SemaphoreType.DMA((phases,)),
            pltpu.SemaphoreType.DMA((phases,)),
        ],
        compiler_params=pltpu.CompilerParams(
            collective_id=0, has_side_effects=True, vmem_limit_bytes=60 * 1024 * 1024
        ),
        cost_estimate=pl.CostEstimate(
            flops=2 * blocks * NBR * BLOCK * BLOCK * (BLOCK + 2 * rows),
            bytes_accessed=2**20, transcendentals=0,
        ),
    )(
        send_order, recv_slot, neighbours.T, want.reshape(regions, CAPACITY).T, enc_feat,
        edge_src, edge_dst, conductance, w_in_h, w_in_m, jnp.swapaxes(w_out, 1, 2), bias_in, ln_gain, ln_shift, w_read.reshape(1, rows),
    )
    return hidden, pressure.reshape(nodes)


def solution(mesh):
    return jax.shard_map(
        on_device,
        mesh=mesh,
        in_specs=(
            P("feat", "region"),
            P("region", None),
            P("region", None),
            P("region", None, None),
            P("region", None),
            P("region", None, None),
            P("region", None, None),
            P("region", None, None),
            P(None, "feat", None),
            P(None, "feat", None),
            P(None, "feat"),
            P(None, None, "feat"),
            P(None, "feat"),
            P(None, "feat"),
            P("feat"),
        ),
        out_specs=(P("feat", "region"), P("region")),
        check_vma=False,
    )
```

```python
import functools

import jax
import jax.numpy as jnp
from jax import lax
from jax.experimental import pallas as pl
from jax.experimental.pallas import tpu as pltpu
from jax.sharding import PartitionSpec as P

BLOCK = 128
NBR = 8
CAPACITY = 4
LAYERS = 2
MESH = pl.DeviceIdType.MESH
NT = (((1,), (1,)), ((), ()))


def wait_bytes(ref, sem):
    pltpu.make_async_copy(ref, ref, sem).wait()


def network_kernel(
    order_hbm, slot_hbm, nbr_hbm, want_hbm, enc_hbm, src_hbm, dst_hbm, cond_hbm,
    w_in_h_hbm, w_in_m_hbm, w_out_hbm, bias_hbm, gain_hbm, shift_hbm, read_hbm,
    hidden, pressure,
    send_order, recv_slot, neighbours, want_row, want_out, inverse, slot_of,
    w_in_h, w_in_m, w_out, bias_in, ln_gain, ln_shift, w_read,
    enc, edge_src, edge_dst, cond, enc_stage, enc_in, want_in, want_all, want_smem,
    state0, ext0, ext1, halo0, halo1, tiles, message0, message1, x0, x1, renewed,
    exports1, others1, final, press_stage, press_in,
    w_stage, w_all, v_rows, v_stage, v_all, v_wide, w_out_all,
    local_sem, send_sem, recv_sem,
):
    regions = lax.axis_size("region")
    feats = lax.axis_size("feat")
    me = lax.axis_index("region")
    my_feat = lax.axis_index("feat")
    blocks = enc.shape[0]
    exports = blocks // 2
    rows = enc.shape[1]
    width = rows * feats
    half = blocks // feats // 2

    sent = []

    def drain():
        for ref, index in sent:
            wait_bytes(ref, send_sem.at[index])

    loads_enc = [
        pltpu.make_async_copy(
            enc_hbm.at[:, block * BLOCK : (block + 1) * BLOCK], enc.at[block], local_sem.at[0]
        )
        for block in range(blocks)
    ]
    small = (
        (order_hbm, send_order), (slot_hbm, recv_slot), (want_hbm, want_row),
        (w_in_h_hbm, w_in_h), (w_in_m_hbm, w_in_m), (w_out_hbm, w_out), (bias_hbm, bias_in),
        (gain_hbm, ln_gain), (shift_hbm, ln_shift), (read_hbm, w_read),
        (src_hbm, edge_src), (dst_hbm, edge_dst), (cond_hbm, cond), (nbr_hbm, neighbours),
    )
    loads = [
        pltpu.make_async_copy(source, target, local_sem.at[1 + at])
        for at, (source, target) in enumerate(small)
    ]
    depth = 8 if regions % 8 == 0 else regions
    lines = regions // depth

    def apart(order, count):
        return lax.rem(count + count // 2 + (order + 1) // 2 * (1 - 2 * lax.rem(order, 2)), count)

    def region_peer(step):
        line = lax.rem(me // depth + apart(step // depth, lines), lines)
        return line * depth + lax.rem(me + apart(lax.rem(step, depth), depth), depth)

    itself = regions - 1

    def feat_peer(step):
        if isinstance(step, int) and step == 0:
            return my_feat
        return lax.rem(my_feat + apart(step - 1, feats), feats)

    barrier = pltpu.get_barrier_semaphore()

    @pl.loop(0, itself, unroll=itself)
    def _(step):
        pl.semaphore_signal(barrier, inc=1, device_id=(region_peer(step), my_feat), device_id_type=MESH)

    @pl.loop(1, feats, unroll=feats - 1)
    def _(step):
        pl.semaphore_signal(barrier, inc=1, device_id=(me, feat_peer(step)), device_id_type=MESH)

    for load in (loads[0], loads[2], loads[1], *loads_enc, *loads[3:]):
        load.start()
    loads[0].wait()
    wait_bytes(enc, local_sem.at[0])

    @pl.loop(0, regions, unroll=regions)
    def _(step):
        enc_stage[step] = enc[send_order[0, region_peer(step)]]

    enc_in[me] = enc_stage[itself]

    loads[2].wait()
    lanes = lax.broadcasted_iota(jnp.int32, (1, BLOCK), 1)

    @pl.loop(0, regions)
    def _(region):
        row = jnp.zeros((1, BLOCK), jnp.int32)
        for panel in range(CAPACITY):
            row = jnp.where(lanes == me * CAPACITY + panel, want_row[panel, region], row)
        want_out[region] = row

    want_in[me] = want_out[me]

    loads[1].wait()
    slots = lax.broadcasted_iota(jnp.int32, inverse.shape, 1)
    found = jnp.zeros(inverse.shape, jnp.int32)
    for source in range(regions):
        found = jnp.where(slots == recv_slot[0, source], source, found)
    inverse[...] = found
    load_slots = pltpu.make_async_copy(inverse, slot_of, local_sem.at[16])
    load_slots.start()

    pl.semaphore_wait(barrier, regions + feats - 2)

    @pl.loop(0, itself, unroll=itself)
    def _(step):
        pltpu.make_async_remote_copy(
            enc_stage.at[step], enc_in.at[me], send_sem.at[0], recv_sem.at[0],
            device_id=(region_peer(step), my_feat), device_id_type=MESH,
        ).start()

    @pl.loop(0, itself, unroll=itself)
    def _(step):
        pltpu.make_async_remote_copy(
            want_out.at[region_peer(step)], want_in.at[me], send_sem.at[1], recv_sem.at[1],
            device_id=(region_peer(step), my_feat), device_id_type=MESH,
        ).start()

    for load in loads[3:10]:
        load.wait()
    eye = (
        lax.broadcasted_iota(jnp.int32, (rows, rows), 0)
        == lax.broadcasted_iota(jnp.int32, (rows, rows), 1)
    )
    mine = pl.ds(pl.multiple_of(my_feat * rows, rows), rows)
    for layer in range(LAYERS):
        w_stage[layer, :, 0:width] = w_in_h[layer]
        w_stage[layer, :, width : 2 * width] = w_in_m[layer]
        w_stage[layer, :, 2 * width :] = w_out[layer]
        w_all[layer, mine, :] = w_stage[layer]
    v_rows[...] = jnp.zeros_like(v_rows)
    v_rows[0:2, :] = bias_in[...]
    v_rows[2:4, :] = ln_gain[...]
    v_rows[4:6, :] = ln_shift[...]
    v_rows[6:7, :] = w_read[...]
    v_stage[...] = jnp.zeros_like(v_stage)
    v_stage[:, 0:8] = lax.dot_general(
        eye.astype(jnp.float32), v_rows[...], NT,
        precision=lax.Precision.HIGHEST, preferred_element_type=jnp.float32,
    )
    v_all[mine, :] = v_stage[...]
    @pl.loop(1, feats, unroll=feats - 1)
    def _(step):
        peer = (me, feat_peer(step))
        pltpu.make_async_remote_copy(
            w_stage, w_all.at[:, mine, :], send_sem.at[2], recv_sem.at[2],
            device_id=peer, device_id_type=MESH,
        ).start()
        pltpu.make_async_remote_copy(
            v_stage, v_all.at[mine, :], send_sem.at[3], recv_sem.at[3],
            device_id=peer, device_id_type=MESH,
        ).start()

    sent.append((enc_stage.at[pl.ds(0, itself)], 0))
    sent.append((want_in.at[pl.ds(0, regions - 1)], 1))
    sent.append((w_all.at[:, pl.ds(0, width - rows), :], 2))
    sent.append((v_all.at[pl.ds(0, width - rows), :], 3))

    for load in loads[10:]:
        load.wait()

    def build_tiles(block):
        pores = lax.broadcasted_iota(jnp.int32, (BLOCK, BLOCK), 0)
        for column in range(NBR):
            src = edge_src[block, column : column + 1, :]
            dst = edge_dst[block, column : column + 1, :]
            weight = cond[block, column : column + 1, :].astype(jnp.float32)
            src_hot = jnp.where(pores == src, 1.0, 0.0).astype(jnp.bfloat16)
            dst_hot = jnp.where(pores == dst, weight, 0.0).astype(jnp.bfloat16)
            tiles[block, column * BLOCK : (column + 1) * BLOCK, :] = lax.dot_general(
                src_hot, dst_hot, NT, preferred_element_type=jnp.float32
            ).astype(jnp.bfloat16)

    early = blocks // 8

    @pl.loop(0, early, unroll=min(4, early))
    def _(block):
        build_tiles(block)

    wait_bytes(enc_in.at[pl.ds(0, regions - 1)], recv_sem.at[0])

    load_slots.wait()

    def place(slot):
        value = enc_in[slot_of[0, slot]]
        state0[slot] = value
        ext0[slot] = value

    pl.loop(exports, blocks, unroll=exports)(place)

    wait_bytes(want_in.at[pl.ds(0, regions - 1)], recv_sem.at[1])
    wants = want_in[0]
    for region in range(1, regions):
        wants = wants + want_in[region]
    want_all[...] = wants
    to_smem = pltpu.make_async_copy(want_all, want_smem, local_sem.at[15])
    to_smem.start()
    to_smem.wait()

    def stage_halo(step, source, first, halo):
        region = region_peer(step)
        for panel in range(CAPACITY):
            entry = want_smem[0, region * CAPACITY + panel]
            halo[step, panel] = source[first + entry]

    def send_halo(step, halo, ext, index):
        pltpu.make_async_remote_copy(
            halo.at[step], ext.at[pl.ds(blocks + me * CAPACITY, CAPACITY)],
            send_sem.at[index], recv_sem.at[index],
            device_id=(region_peer(step), my_feat), device_id_type=MESH,
        ).start()

    def exchange_halo(source, first, halo, ext, index):
        @pl.loop(0, itself, unroll=itself)
        def _(step):
            stage_halo(step, source, first, halo)
            send_halo(step, halo, ext, index)

        sent.append((halo.at[pl.ds(0, itself)], index))
        stage_halo(itself, source, first, halo)
        for panel in range(CAPACITY):
            ext[blocks + me * CAPACITY + panel] = halo[itself, panel]

    exchange_halo(state0, exports, halo0, ext0, 4)

    def share(side):
        def from_peer(step):
            return pl.ds(side * exports + feat_peer(step) * half, half)

        return from_peer

    def to_owner(source, x, side, first_row, index):
        into = pl.ds(pl.multiple_of(first_row + my_feat * rows, rows), rows)
        where = share(side)

        @pl.loop(1, feats, unroll=feats - 1)
        def _(step):
            pltpu.make_async_remote_copy(
                source.at[where(step)], x.at[side, :, into, :],
                send_sem.at[index], recv_sem.at[index],
                device_id=(me, feat_peer(step)), device_id_type=MESH,
            ).start()

        sent.append((state0.at[pl.ds(0, half * (feats - 1))], index))
        x[side, :, into, :] = source[where(0)]

    pl.loop(0, exports, unroll=exports)(place)
    to_owner(state0, x0, 1, 0, 5)
    to_owner(state0, x0, 0, 0, 6)

    @pl.loop(early, blocks, unroll=min(4, early))
    def _(block):
        build_tiles(block)

    wait_bytes(w_all.at[:, pl.ds(0, width - rows), :], recv_sem.at[2])
    wait_bytes(v_all.at[pl.ds(0, width - rows), :], recv_sem.at[3])
    eye_all = (
        lax.broadcasted_iota(jnp.int32, (width, width), 0)
        == lax.broadcasted_iota(jnp.int32, (width, width), 1)
    ).astype(jnp.bfloat16)
    for layer in range(LAYERS):
        w_out_all[layer] = lax.dot_general(
            eye_all, w_all[layer, :, 2 * width :], NT, preferred_element_type=jnp.float32
        ).astype(jnp.bfloat16)

    for vector in range(7):
        v_wide[vector] = jnp.broadcast_to(v_all[:, vector : vector + 1], (width, BLOCK))

    def wide(vector):
        return jnp.concatenate([v_wide[vector]] * half, axis=1)

    def aggregate(ext, message, side):
        @pl.loop(side * exports, (side + 1) * exports, unroll=min(16, exports))
        def _(block):
            sources = jnp.concatenate(
                [ext[neighbours[column, block]] for column in range(NBR)], axis=1
            )
            message[block] = jnp.dot(
                sources, tiles[block], preferred_element_type=jnp.float32
            ).astype(jnp.bfloat16)

    def update(x, side, layer):
        both = jnp.concatenate([x[side, j] for j in range(half)], axis=1)
        pre = jnp.dot(w_all[layer, :, 0 : 2 * width], both, preferred_element_type=jnp.float32)
        inner = jnp.maximum(pre + wide(layer), 0.0).astype(jnp.bfloat16)
        y = jnp.dot(w_out_all[layer], inner, preferred_element_type=jnp.float32)
        mean = jnp.mean(y, axis=0, keepdims=True)
        shifted = y - mean
        var = jnp.mean(shifted * shifted, axis=0, keepdims=True)
        normed = shifted * lax.rsqrt(var + 1e-05)
        change = normed * wide(2 + layer) + wide(4 + layer)
        return (both[0:width].astype(jnp.float32) + change).astype(jnp.bfloat16)

    def wait_owner(x, side, index):
        wait_bytes(x.at[side, :, pl.ds(0, width - rows), :], recv_sem.at[index])

    def give_back(x, into, side, first, index):
        where = pl.ds(first + my_feat * half, half)

        def part(step):
            return x.at[side, :, pl.ds(pl.multiple_of(feat_peer(step) * rows, rows), rows), :]

        @pl.loop(1, feats, unroll=feats - 1)
        def _(step):
            pltpu.make_async_remote_copy(
                part(step), into.at[where], send_sem.at[index], recv_sem.at[index],
                device_id=(me, feat_peer(step)), device_id_type=MESH,
            ).start()

        sent.append((state0.at[pl.ds(0, half * (feats - 1))], index))
        into[where] = part(0)[...]

    def wait_back(into, index):
        wait_bytes(into.at[pl.ds(0, half * (feats - 1))], recv_sem.at[index])

    halo_bytes = pl.ds(0, (regions - 1) * CAPACITY)
    wait_bytes(ext0.at[halo_bytes], recv_sem.at[4])
    for side in (1, 0):
        aggregate(ext0, message0, side)
        to_owner(message0, x0, side, width, 8 - side)
    for side, into in ((1, exports1), (0, others1)):
        wait_owner(x0, side, 6 - side)
        wait_owner(x0, side, 8 - side)
        new = update(x0, side, 0)
        for j in range(half):
            x1[side, j, 0:width, :] = new[:, j * BLOCK : (j + 1) * BLOCK]
        give_back(x1, into, side, 0, 10 - side)

    wait_back(exports1, 9)
    exchange_halo(exports1, 0, halo1, ext1, 11)
    ext1[pl.ds(exports, exports)] = exports1[...]
    wait_back(others1, 10)
    ext1[pl.ds(0, exports)] = others1[...]
    wait_bytes(ext1.at[halo_bytes], recv_sem.at[11])
    for side in (1, 0):
        aggregate(ext1, message1, side)
        to_owner(message1, x1, side, width, 13 - side)
    for side in (1, 0):
        wait_owner(x1, side, 13 - side)
        new = update(x1, side, 1)
        scaled = wide(6) * new.astype(jnp.float32)
        total = jnp.sum(scaled, axis=0, keepdims=True)
        for j in range(half):
            renewed[side, j] = new[:, j * BLOCK : (j + 1) * BLOCK]
            press_stage[0, side * half + j : side * half + j + 1, :] = (
                total[:, j * BLOCK : (j + 1) * BLOCK]
            )
        give_back(renewed, final, side, side * exports, 15 - side)

    @pl.loop(1, feats, unroll=feats - 1)
    def _(step):
        pltpu.make_async_remote_copy(
            press_stage, press_in.at[pl.ds(my_feat, 1)], send_sem.at[16], recv_sem.at[16],
            device_id=(me, feat_peer(step)), device_id_type=MESH,
        ).start()

    sent.append((press_in.at[pl.ds(0, feats - 1)], 16))
    press_in[pl.ds(my_feat, 1)] = press_stage[...]
    wait_back(final, 14)
    wait_back(final, 15)
    for block in range(blocks):
        hidden[:, block * BLOCK : (block + 1) * BLOCK] = final[block]
    wait_bytes(press_in.at[pl.ds(0, feats - 1)], recv_sem.at[16])
    for feat in range(feats):
        for side in range(2):
            first = side * exports + feat * half
            pressure[first : first + half, :] = press_in[feat, side * half : (side + 1) * half, :]

    drain()


def on_device(
    enc_feat, send_order, recv_slot, want, neighbours, edge_src, edge_dst, conductance,
    w_in_h, w_in_m, bias_in, w_out, ln_gain, ln_shift, w_read,
):
    regions = lax.axis_size("region")
    feats = lax.axis_size("feat")
    rows, nodes = enc_feat.shape
    blocks = neighbours.shape[0]
    exports = blocks // 2
    width = rows * feats
    own = blocks // feats
    half = own // 2
    panels = regions * CAPACITY
    bf16, f32, i32 = jnp.bfloat16, jnp.float32, jnp.int32
    vmem = pl.BlockSpec(memory_space=pltpu.VMEM)
    phases = 17
    hidden, pressure = pl.pallas_call(
        network_kernel,
        out_shape=(
            jax.ShapeDtypeStruct((rows, nodes), bf16),
            jax.ShapeDtypeStruct((blocks, BLOCK), f32),
        ),
        in_specs=[pl.BlockSpec(memory_space=pltpu.HBM)] * 15,
        out_specs=(vmem, vmem),
        scratch_shapes=[
            pltpu.SMEM((1, blocks), i32),
            pltpu.SMEM((1, regions), i32),
            pltpu.SMEM((NBR, blocks), i32),
            pltpu.SMEM((CAPACITY, regions), i32),
            pltpu.VMEM((regions, 1, BLOCK), i32),
            pltpu.VMEM((1, BLOCK), i32),
            pltpu.SMEM((1, BLOCK), i32),
            pltpu.VMEM((LAYERS, rows, width), bf16),
            pltpu.VMEM((LAYERS, rows, width), bf16),
            pltpu.VMEM((LAYERS, rows, width), bf16),
            pltpu.VMEM((LAYERS, rows), f32),
            pltpu.VMEM((LAYERS, rows), f32),
            pltpu.VMEM((LAYERS, rows), f32),
            pltpu.VMEM((1, rows), f32),
            pltpu.VMEM((blocks, rows, BLOCK), bf16),
            pltpu.VMEM((blocks, NBR, BLOCK), i32),
            pltpu.VMEM((blocks, NBR, BLOCK), i32),
            pltpu.VMEM((blocks, NBR, BLOCK), bf16),
            pltpu.VMEM((regions, rows, BLOCK), bf16),
            pltpu.VMEM((regions, rows, BLOCK), bf16),
            pltpu.VMEM((regions, 1, BLOCK), i32),
            pltpu.VMEM((1, BLOCK), i32),
            pltpu.SMEM((1, BLOCK), i32),
            pltpu.VMEM((blocks, rows, BLOCK), bf16),
            pltpu.VMEM((blocks + panels, rows, BLOCK), bf16),
            pltpu.VMEM((blocks + panels, rows, BLOCK), bf16),
            pltpu.VMEM((regions, CAPACITY, rows, BLOCK), bf16),
            pltpu.VMEM((regions, CAPACITY, rows, BLOCK), bf16),
            pltpu.VMEM((blocks, NBR * BLOCK, BLOCK), bf16),
            pltpu.VMEM((blocks, rows, BLOCK), bf16),
            pltpu.VMEM((blocks, rows, BLOCK), bf16),
            pltpu.VMEM((2, half, 2 * width, BLOCK), bf16),
            pltpu.VMEM((2, half, 2 * width, BLOCK), bf16),
            pltpu.VMEM((2, half, width, BLOCK), bf16),
            pltpu.VMEM((exports, rows, BLOCK), bf16),
            pltpu.VMEM((exports, rows, BLOCK), bf16),
            pltpu.VMEM((blocks, rows, BLOCK), bf16),
            pltpu.VMEM((1, own, BLOCK), f32),
            pltpu.VMEM((feats, own, BLOCK), f32),
            pltpu.VMEM((LAYERS, rows, 3 * width), bf16),
            pltpu.VMEM((LAYERS, width, 3 * width), bf16),
            pltpu.VMEM((8, rows), f32),
            pltpu.VMEM((rows, BLOCK), f32),
            pltpu.VMEM((width, BLOCK), f32),
            pltpu.VMEM((7, width, BLOCK), f32),
            pltpu.VMEM((LAYERS, width, width), bf16),
            pltpu.SemaphoreType.DMA((17,)),
            pltpu.SemaphoreType.DMA((phases,)),
            pltpu.SemaphoreType.DMA((phases,)),
        ],
        compiler_params=pltpu.CompilerParams(
            collective_id=0, has_side_effects=True, vmem_limit_bytes=60 * 1024 * 1024
        ),
        cost_estimate=pl.CostEstimate(
            flops=2 * blocks * NBR * BLOCK * BLOCK * (BLOCK + 2 * rows),
            bytes_accessed=2**20, transcendentals=0,
        ),
    )(
        send_order, recv_slot, neighbours.T, want.reshape(regions, CAPACITY).T, enc_feat,
        edge_src, edge_dst, conductance, w_in_h, w_in_m, jnp.swapaxes(w_out, 1, 2), bias_in, ln_gain, ln_shift, w_read.reshape(1, rows),
    )
    return hidden, pressure.reshape(nodes)


def solution(mesh):
    return jax.shard_map(
        on_device,
        mesh=mesh,
        in_specs=(
            P("feat", "region"),
            P("region", None),
            P("region", None),
            P("region", None, None),
            P("region", None),
            P("region", None, None),
            P("region", None, None),
            P("region", None, None),
            P(None, "feat", None),
            P(None, "feat", None),
            P(None, "feat"),
            P(None, None, "feat"),
            P(None, "feat"),
            P(None, "feat"),
            P("feat"),
        ),
        out_specs=(P("feat", "region"), P("region")),
        check_vma=False,
    )
```
